512 devices in a mesh: ew: 32 (over z, x), ns: 16 (over y, core).
Axes of the slice: x: 4, y: 8, z: 8, core: 2. Of those that a mesh axis runs over, the one named last changes fastest.
Arguments:
- grid: bfloat16 [32, 2, 1280, 5152], P(None, None, 'ns', 'ew'), may hold values from -6 to 6
- band_rows: int32 [1280], replicated, may hold values from 0 to 1279, each once
- wave_pairs: int32 [16], replicated, may hold values from 0 to 323, as said below
- packer_order: int32 [32], replicated, may hold values from 0 to 31, each once
- field_bits: int32 [4], replicated, may hold values from 10 to 14
- field_power: float32 [4], replicated, may hold values from -0.6 to 0.6
- legendre: float32 [16, 1280, 649], P('ns'), may hold values from -0.15625 to 0.15625
Outputs:
- packed: float32 [32, 16, 2, 649], P('ew', 'ns')
The draws below stay inside these ranges and needn't reach their ends.
Inputs may be any that keep to these rules, and one draw needn't show every extreme that they name: `wave_pairs`: distinct values.
All inputs are finite; a program needn't handle non-finite values.
Results may differ from the reference program's by a relative error of at most 0.0003.
Values sent between devices are 32-bit elements; how exact they have to be, the bound alone decides.
A program may use at most 64 MiB of HBM per device.

```python
import jax
import jax.numpy as jnp
from jax import lax

NLATH = 1280
TRUNC = 647
FIELDS = 4
FL = 32
LEV = 8
PAIRS = 16
NCOL = 649
PADW = 5152


def draw_wave_pairs(key, part):
    halfway = (TRUNC + 1) // 2
    first_key = jax.random.fold_in(key, 11)
    second_key = jax.random.fold_in(key, 23)
    inner = 1 + jax.random.permutation(first_key, halfway - 2)[:PAIRS - 2]
    values = jnp.concatenate([jnp.array([0, halfway - 1], dtype=jnp.int32), inner.astype(jnp.int32)])
    order = jax.random.permutation(second_key, PAIRS)
    return values[order].astype(jnp.int32)


def plant(values, key, low, largest):
    index_at = [jax.random.randint(jax.random.fold_in(key, axis), (), 0, length) for axis, length in enumerate(values.shape)]
    widest = values.shape.index(max(values.shape))
    neighbour = index_at[:widest] + [(index_at[widest] + 1) % values.shape[widest]] + index_at[widest + 1:]
    return values.at[tuple(index_at)].set(low).at[tuple(neighbour)].set(largest)


def steps_of(key, extent, cuts, least, high):
    gain, own = 1.0, jax.random.fold_in(key, 6)
    for position, parts in cuts:
        steps = jnp.exp(jax.random.uniform(jax.random.fold_in(own, position), (parts,), jnp.float32, least / len(cuts), high / len(cuts)))
        gain = gain * jnp.repeat(steps, extent[position] // parts).reshape([-1 if axis == position else 1 for axis in range(len(extent))])
    return gain


def noise(key, dims, scale, reach, cuts=(), kind=jnp.bfloat16):
    gain = steps_of(key, dims, cuts, -0.22, 0.18) if cuts else 1.0
    entries = jax.random.normal(key, dims, jnp.float32) * scale * gain
    return jnp.minimum(jnp.maximum(entries, -reach), reach).astype(kind)


def setup_inputs(seed: int = 0) -> dict:
    splits = jax.random.split(jax.random.key(seed), 8)
    return {
        "grid": noise(splits[0], (FL, 2, NLATH, PADW), 1.0, 6.0, ((2, 16), (3, 32))),
        "band_rows": jax.random.permutation(splits[1], NLATH).astype(jnp.int32),
        "wave_pairs": draw_wave_pairs(jax.random.fold_in(splits[7], 71), 0),
        "packer_order": jax.random.permutation(splits[3], FL).astype(jnp.int32),
        "field_bits": plant(jax.random.randint(splits[4], (FIELDS,), 10, 15), jax.random.fold_in(splits[4], 1), 10, 14).astype(jnp.int32),
        "field_power": jnp.clip(jax.random.uniform(splits[5], (FIELDS,), jnp.float32, -0.6, 0.6), -0.6, 0.6),
        "legendre": noise(splits[6], (PAIRS, NLATH, NCOL), NLATH ** -0.5, 0.15625, ((0, 16),), jnp.float32),
    }


def cycle_table(lat_ids, first_point, point_count, wave_list, truncation):
    lengths = 20 + 4 * lat_ids
    points = first_point + jnp.arange(point_count, dtype=jnp.int32)
    numbers = jnp.stack([wave_list, truncation - wave_list], 1).reshape(-1)
    product = (numbers[None, None, :] * points[None, :, None]) % lengths[:, None, None]
    length_f = lengths.astype(jnp.float32)[:, None, None]
    angles = product.astype(jnp.float32) * (6.283185307179586 / length_f)
    inside = points[None, :, None] < lengths[:, None, None]
    factor = jnp.where(inside, 1.0 / length_f, jnp.float32(0.0))
    trig_values = jnp.stack([jnp.cos(angles) * factor, -jnp.sin(angles) * factor], -1)
    return trig_values.reshape(lat_ids.shape[0], point_count, -1)


def coefficients(ordered, legendre, wave_list, truncation, powers):
    symmetric = ordered[:, 0] + ordered[:, 1]
    antisym = ordered[:, 0] - ordered[:, 1]
    slots, nlat, width = symmetric.shape
    pcount = width // 4
    stacked = jnp.concatenate([symmetric.reshape(slots, nlat, pcount, 4), antisym.reshape(slots, nlat, pcount, 4)], -1)
    result = jnp.einsum("prc,frpq->fpqc", legendre.astype(jnp.float32), stacked.astype(jnp.float32), precision=lax.Precision.HIGHEST)
    columns = jnp.arange(legendre.shape[2], dtype=jnp.int32)[None, :]
    wavenum = wave_list[:, None]
    first_part = columns <= truncation - wavenum
    shifted = columns - (truncation - wavenum + 1)
    even_parity = jnp.where(first_part, columns % 2 == 0, shifted % 2 == 0)
    halves = []
    for e in (0, 1):
        chosen = jnp.where(first_part, jnp.where(even_parity, result[:, :, e], result[:, :, 4 + e]), jnp.where(even_parity, result[:, :, 2 + e], result[:, :, 6 + e]))
        halves.append(chosen)
    coefficient = jnp.stack(halves, 2)
    degree = jnp.where(first_part, wavenum + columns, columns - 1).astype(jnp.float32)
    logs = jnp.log(degree * (degree + 1.0) + 2.0)
    weight = jnp.exp(powers[:, None, None] * logs[None, :, :])
    return coefficient * weight[:, :, None, :]


def slot_settings(slot_fields, field_bits, field_power, levels):
    field_type = slot_fields // levels
    onehot = field_type[:, None] == jnp.arange(field_bits.shape[0], dtype=jnp.int32)[None, :]
    powers = jnp.sum(jnp.where(onehot, field_power[None, :], jnp.float32(0.0)), -1)
    bit_count = jnp.sum(jnp.where(onehot, field_bits[None, :], 0), -1).astype(jnp.float32)
    return powers, (jnp.exp2(bit_count) - 1.0) / 4096.0


def pack_values(scaled, lowest, highest, spread):
    span = highest - lowest + 1e-6
    return (scaled - lowest[:, None, None, None]) / span[:, None, None, None] * spread[:, None, None, None]


def reference(grid, band_rows, wave_pairs, packer_order, field_bits, field_power, legendre):
    point_slots = grid.shape[3]

    def one_row(row):
        trig_values = cycle_table(band_rows[row][None], jnp.int32(0), point_slots, wave_pairs, TRUNC)[0]
        values = lax.dynamic_index_in_dim(grid, row, 2, keepdims=False).astype(jnp.float32)
        return jnp.einsum("fhk,kc->fhc", values, trig_values, precision=lax.Precision.HIGHEST)

    fourier = lax.map(one_row, jnp.arange(NLATH, dtype=jnp.int32))
    fourier = jnp.transpose(fourier, (1, 2, 0, 3))
    ordered = fourier[packer_order]
    powers, spread = slot_settings(packer_order, field_bits, field_power, LEV)
    scaled = coefficients(ordered, legendre, wave_pairs, TRUNC, powers)
    highest = jnp.max(scaled, axis=(1, 2, 3))
    lowest = jnp.min(scaled, axis=(1, 2, 3))
    return pack_values(scaled, lowest, highest, spread)
```

```python
import functools

import jax
import jax.numpy as jnp
import numpy as np
from jax import lax
from jax.experimental import pallas as pl
from jax.experimental.pallas import tpu as pltpu
from jax.sharding import PartitionSpec as P

MESH = pl.DeviceIdType.MESH
NX = 4
NZ = 8
NS = 16
CH = 16
F32 = jnp.float32
BF16 = jnp.bfloat16


def _fit(function, terms):
    z = 0.125 + 0.125 * np.cos(np.pi * (np.arange(200) + 0.5) / 200)
    cheb = np.polynomial.chebyshev.Chebyshev.fit(z, function(np.sqrt(z)), terms - 1, domain=[0, 0.25])
    return [float(v) for v in cheb.convert(kind=np.polynomial.Polynomial).coef]


COS = _fit(lambda t: np.cos(2 * np.pi * t), 8)
SIN = _fit(lambda t: np.sin(2 * np.pi * t) / t, 8)


def _horner(coefs, z):
    total = jnp.full_like(z, coefs[-1])
    for c in coefs[-2::-1]:
        total = total * z + c
    return total


def _cos_sin(product, length, inverse):
    rest = product - jnp.round(product * inverse) * length
    t = rest * inverse
    z = t * t
    return _horner(COS, z), t * _horner(SIN, z)


def kernel(
    truncation, levels,
    band_s, waves_s, order_s, bits_s, power_s, grid_hbm, leg_hbm,
    out_ref,
    gridv, legv, leghi, leglo, xf, w, cs, sbuf, rx, zbuf, rz, obuf, ybuf, ry, rmm,
    grid_sem, leg_sem, xs_sem, xr_sem, zs_sem, zr_sem, ys_sem, yr_sem, ms_sem, mr_sem,
):
    ew, ns = lax.axis_index("ew"), lax.axis_index("ns")
    x, z = lax.rem(ew, NX), lax.div(ew, NX)
    rows = gridv.shape[2]
    points = gridv.shape[3]
    chunks = rows // CH

    grid_copy = pltpu.make_async_copy(grid_hbm, gridv, grid_sem)
    grid_copy.start()
    leg_copy = pltpu.make_async_copy(leg_hbm, legv, leg_sem)
    leg_copy.start()

    barrier = pltpu.get_barrier_semaphore()
    for d in range(1, NX):
        pl.semaphore_signal(barrier, inc=1, device_id={"ew": z * NX + lax.rem(x + d, NX)}, device_id_type=MESH)
    for d in range(1, NZ):
        pl.semaphore_signal(barrier, inc=1, device_id={"ew": lax.rem(z + d, NZ) * NX + x}, device_id_type=MESH)
    for d in range(1, NS):
        pl.semaphore_signal(barrier, inc=1, device_id={"ns": lax.rem(ns + d, NS)}, device_id_type=MESH)

    w[...] = jnp.zeros_like(w)
    xf[...] = jnp.zeros_like(xf)

    lane = lax.broadcasted_iota(jnp.int32, (16, 128), 1)
    sub16 = lax.broadcasted_iota(jnp.int32, (16, 128), 0)
    pair_of = (lane & 63) >> 2
    wave = jnp.zeros((16, 128), jnp.int32)
    for p in range(16):
        wave = jnp.where(pair_of == p, waves_s[p], wave)
    wave = jnp.where((lane & 2) == 0, wave, truncation - wave).astype(F32)
    imaginary = (lane & 1) == 1
    low_half = lane < 64
    first = ew * points
    product_a = wave * (first + 16 * sub16).astype(F32)
    product_b = wave * sub16.astype(F32)
    point0 = (first + sub16).astype(F32)
    point_end = (first + points).astype(F32)

    grid_copy.wait()

    def chunk(c, _):
        def convert(zz, _):
            for xx in range(NX):
                field = order_s[zz * NX + xx]
                for h in range(2):
                    at = pl.multiple_of((h * 32 + xx * NZ + zz) * CH, CH)
                    block = gridv[field, h, pl.ds(pl.multiple_of(c * CH, CH), CH), :].astype(F32)
                    xf[0, pl.ds(at, CH), :] = block[:, 0:128]
                    xf[1, pl.ds(at, CH), 0 : points - 128] = block[:, 128:points]
            return 0

        lax.fori_loop(0, NZ, convert, 0)

        def half(g, _):
            for j in range(4):
                row0 = g * 8 + j
                band0 = band_s[ns * rows + c * CH + row0]
                band1 = band_s[ns * rows + c * CH + row0 + 4]
                length = jnp.where(low_half, 20 + 4 * band0, 20 + 4 * band1).astype(F32)
                inverse = 1.0 / length
                cos_a, sin_a = _cos_sin(product_a, length, inverse)
                cos_b, sin_b = _cos_sin(product_b, length, inverse)
                cs[j, 0] = jnp.where(imaginary, -sin_a, cos_a) * inverse
                cs[j, 1] = jnp.where(imaginary, cos_a, sin_a) * inverse
                end = jnp.minimum(length, point_end) - point0
                for a in range(11):
                    value = cs[j, 0, a : a + 1, :] * cos_b - cs[j, 1, a : a + 1, :] * sin_b
                    value = jnp.where(end > 16.0 * a, value, 0.0)
                    high = value.astype(BF16)
                    low = (value - high.astype(F32)).astype(BF16)
                    w[j, 16 * a : 16 * a + 16, 0:128] = high
                    w[j, 16 * a : 16 * a + 16, 128:256] = low
                sides = []
                for side in range(2):
                    x0 = xf[side, pl.ds(row0, 64, stride=CH), :].astype(BF16)
                    x1 = xf[side, pl.ds(row0 + 4, 64, stride=CH), :].astype(BF16)
                    sides.append(jnp.concatenate([x0, x1], 0))
                both = jnp.dot(jnp.concatenate(sides, 1), w[j], preferred_element_type=F32)
                both = both[:, :128] + both[:, 128:]
                out = jnp.where(lax.broadcasted_iota(jnp.int32, (64, 128), 1) < 64, both[:64], both[64:])
                for h in range(2):
                    for xx in range(NX):
                        sbuf[c, xx, pl.ds(g * 8 + h * 4 + j, NZ, stride=CH), :] = out[h * 32 + xx * NZ : h * 32 + xx * NZ + NZ]
            return 0

        lax.fori_loop(0, CH // 8, half, 0)

        @pl.when(c == 0)
        def _():
            pl.semaphore_wait(barrier, NX - 1 + NZ - 1 + NS - 1)

        for d in range(1, NX):
            x_copy(c, d).start()
        return 0

    def x_copy(c, d):
        to = lax.rem(x + d, NX)
        return pltpu.make_async_remote_copy(
            src_ref=sbuf.at[c, to], dst_ref=rx.at[c, d - 1],
            send_sem=xs_sem.at[c, d - 1], recv_sem=xr_sem.at[c, d - 1],
            device_id={"ew": z * NX + to}, device_id_type=MESH)

    def z_copy(c, d):
        to = lax.rem(z + d, NZ)
        return pltpu.make_async_remote_copy(
            src_ref=zbuf.at[c, pl.ds(pl.multiple_of(to * CH, CH), CH)], dst_ref=rz.at[c, d - 1],
            send_sem=zs_sem.at[c, d - 1], recv_sem=zr_sem.at[c, d - 1],
            device_id={"ew": to * NX + x}, device_id_type=MESH)

    def y_copy(d):
        to = lax.rem(ns + d, NS)
        return pltpu.make_async_remote_copy(
            src_ref=ybuf.at[to], dst_ref=ry.at[ns],
            send_sem=ys_sem.at[d - 1], recv_sem=yr_sem.at[d - 1],
            device_id={"ns": to}, device_id_type=MESH)

    def m_copy(d):
        to = lax.rem(ns + d, NS)
        return pltpu.make_async_remote_copy(
            src_ref=rmm.at[0], dst_ref=rmm.at[d],
            send_sem=ms_sem.at[d - 1], recv_sem=mr_sem.at[d - 1],
            device_id={"ns": to}, device_id_type=MESH)

    lax.fori_loop(0, chunks, chunk, 0)

    leg_copy.wait()

    def split(i, _):
        at = pl.ds(pl.multiple_of(i * 80, 16), 80)
        value = legv[at, :]
        high = value.astype(BF16)
        leghi[at, :] = high
        leglo[at, :] = (value - high.astype(F32)).astype(BF16)
        return 0

    lax.fori_loop(0, legv.shape[0] // 80, split, 0)

    def second(c, _):
        for d in range(1, NX):
            x_copy(c, d).wait_recv()
        zbuf[c] = sbuf[c, x] + rx[c, 0] + rx[c, 1] + rx[c, 2]
        for d in range(1, NZ):
            z_copy(c, d).start()
        return 0

    lax.fori_loop(0, chunks, second, 0)

    sub8 = lax.broadcasted_iota(jnp.int32, (8, 128), 0)
    lane8 = lax.broadcasted_iota(jnp.int32, (8, 128), 1)
    obuf[...] = jnp.zeros_like(obuf)

    def third(c, _):
        for d in range(1, NZ):
            z_copy(c, d).wait_recv()
        total = zbuf[c, pl.ds(pl.multiple_of(z * CH, CH), CH)]
        for d in range(NZ - 1):
            total = total + rz[c, d]
        for g in range(CH // 8):
            o = total[g * 8 : g * 8 + 8]
            r = pltpu.roll(o, 4, 0)
            o = jnp.where(sub8 < 4, o + r, r - o)
            r = pltpu.roll(pltpu.roll(o, 4, 0), 64, 1)
            o = jnp.where((sub8 < 4) == (lane8 < 64), o, r)
            obuf[pl.ds(pl.multiple_of(c * CH + g * 8, 8), 8), :] = o
        return 0

    lax.fori_loop(0, chunks, third, 0)

    turned = obuf[...].T
    for p in range(NS):
        ybuf[p] = jnp.concatenate([turned[4 * p : 4 * p + 4], turned[64 + 4 * p : 68 + 4 * p]], 0)
    for d in range(1, NS):
        y_copy(d).start()
    ry[ns] = ybuf[ns]

    columns = legv.shape[1]
    column = lax.broadcasted_iota(jnp.int32, (2, columns), 1)
    wavenum = waves_s[ns]
    in_first = column <= truncation - wavenum
    shifted = jnp.where(in_first, column, column - (truncation - wavenum + 1))
    even = (shifted & 1) == 0
    degree = jnp.where(in_first, wavenum + column, column - 1).astype(F32)
    field_type = lax.div(order_s[ew], levels)
    power, bits = power_s[0], bits_s[0]
    for t in range(1, bits_s.shape[0]):
        power = jnp.where(field_type == t, power_s[t], power)
        bits = jnp.where(field_type == t, bits_s[t], bits)
    weight = jnp.exp(power * jnp.log(degree * (degree + 1.0) + 2.0))
    spread = (lax.shift_left(jnp.int32(1), bits) - 1).astype(F32) * (1.0 / 4096.0)

    for d in range(1, NS):
        y_copy(d).wait_recv()
    pieces = [None] * (rows * NS // 128)
    for i in range(NS):
        at, off = divmod(i * rows, 128)
        value = ry[i] if off == 0 else pltpu.roll(ry[i], off, 1)
        if off + rows <= 128:
            parts = [(at, value)]
        else:
            parts = [(at, jnp.where(lane8 >= off, value, 0.0)), (at + 1, jnp.where(lane8 < off, value, 0.0))]
        for k, v in parts:
            pieces[k] = v if pieces[k] is None else pieces[k] + v
    stacked = jnp.concatenate(pieces, 1)
    high = stacked.astype(BF16).astype(F32)
    both = jnp.concatenate([high, stacked - high], 0).astype(BF16)
    by_high = jnp.dot(both, leghi[...], preferred_element_type=F32)
    by_low = jnp.dot(both, leglo[...], preferred_element_type=F32)
    result = by_high[:8] + by_high[8:] + by_low[:8]

    chosen = jnp.where(
        in_first,
        jnp.where(even, result[0:2], result[4:6]),
        jnp.where(even, result[2:4], result[6:8]),
    )
    scaled = chosen * weight
    most = jnp.max(scaled)
    least = jnp.min(scaled)
    rmm[0] = jnp.where(lane8 < 64, most, -least)
    for d in range(1, NS):
        m_copy(d).start()
    for d in range(1, NS):
        m_copy(d).wait_recv()
    top = rmm[0]
    for d in range(1, NS):
        top = jnp.maximum(top, rmm[d])
    highest = jnp.max(jnp.where(lane8 < 64, top, -jnp.inf))
    lowest = -jnp.max(jnp.where(lane8 < 64, -jnp.inf, top))
    span = highest - lowest + 1e-6
    out_ref[0, 0] = (scaled - lowest) / span * spread

    def sent(c, _):
        for d in range(1, NX):
            x_copy(c, d).wait_send()
        for d in range(1, NZ):
            z_copy(c, d).wait_send()
        return 0

    lax.fori_loop(0, chunks, sent, 0)
    for d in range(1, NS):
        y_copy(d).wait_send()
        m_copy(d).wait_send()


def shards(grid, band_rows, wave_pairs, packer_order, field_bits, field_power, legendre):
    fields, hemis, rows, points = grid.shape
    lats, columns = legendre.shape[1:]
    truncation = columns - 2
    levels = fields // field_bits.shape[0]
    chunks = rows // CH
    smem = pl.BlockSpec(memory_space=pltpu.SMEM)
    hbm = pl.BlockSpec(memory_space=pl.ANY)
    dma = pltpu.SemaphoreType.DMA
    return pl.pallas_call(
        functools.partial(kernel, truncation, levels),
        out_shape=jax.ShapeDtypeStruct((1, 1, 2, columns), F32),
        in_specs=[smem] * 5 + [hbm] * 2,
        out_specs=pl.BlockSpec(memory_space=pltpu.VMEM),
        scratch_shapes=[
            pltpu.VMEM((fields, hemis, rows, points), BF16),
            pltpu.VMEM((lats, columns), F32),
            pltpu.VMEM((lats, columns), BF16),
            pltpu.VMEM((lats, columns), BF16),
            pltpu.VMEM((2, fields * hemis * CH, 128), F32),
            pltpu.VMEM((4, 256, 256), BF16),
            pltpu.VMEM((4, 2, 16, 128), F32),
            pltpu.VMEM((chunks, NX, NZ * CH, 128), F32),
            pltpu.VMEM((chunks, NX - 1, NZ * CH, 128), F32),
            pltpu.VMEM((chunks, NZ * CH, 128), F32),
            pltpu.VMEM((chunks, NZ - 1, CH, 128), F32),
            pltpu.VMEM((128, 128), F32),
            pltpu.VMEM((NS, 8, 128), F32),
            pltpu.VMEM((NS, 8, 128), F32),
            pltpu.VMEM((NS, 8, 128), F32),
            dma,
            dma,
            dma((chunks, NX - 1)),
            dma((chunks, NX - 1)),
            dma((chunks, NZ - 1)),
            dma((chunks, NZ - 1)),
            dma((NS - 1,)),
            dma((NS - 1,)),
            dma((NS - 1,)),
            dma((NS - 1,)),
        ],
        compiler_params=pltpu.CompilerParams(
            collective_id=0, has_side_effects=True, vmem_limit_bytes=48 * 2**20
        ),
    )(band_rows, wave_pairs, packer_order, field_bits, field_power, grid, legendre.reshape(lats, columns))


def solution(mesh):
    return jax.shard_map(
        shards,
        mesh=mesh,
        in_specs=(P(None, None, "ns", "ew"), P(), P(), P(), P(), P(), P("ns", None, None)),
        out_specs=P("ew", "ns", None, None),
        check_vma=False,
    )
```

```python
import functools

import jax
import jax.numpy as jnp
import numpy as np
from jax import lax
from jax.experimental import pallas as pl
from jax.experimental.pallas import tpu as pltpu
from jax.sharding import PartitionSpec as P

MESH = pl.DeviceIdType.MESH
NX = 4
NZ = 8
NS = 16
CH = 16
F32 = jnp.float32
BF16 = jnp.bfloat16


def _fit(function, terms):
    z = 0.125 + 0.125 * np.cos(np.pi * (np.arange(200) + 0.5) / 200)
    cheb = np.polynomial.chebyshev.Chebyshev.fit(z, function(np.sqrt(z)), terms - 1, domain=[0, 0.25])
    return [float(v) for v in cheb.convert(kind=np.polynomial.Polynomial).coef]


COS = _fit(lambda t: np.cos(2 * np.pi * t), 8)
SIN = _fit(lambda t: np.sin(2 * np.pi * t) / t, 8)


def _horner(coefs, z):
    total = jnp.full_like(z, coefs[-1])
    for c in coefs[-2::-1]:
        total = total * z + c
    return total


def _cos_sin(product, length, inverse):
    rest = product - jnp.round(product * inverse) * length
    t = rest * inverse
    z = t * t
    return _horner(COS, z), t * _horner(SIN, z)


def kernel(
    truncation, levels,
    band_s, waves_s, order_s, bits_s, power_s, grid_hbm, leg_hbm,
    out_ref,
    gridv, legv, leghi, leglo, xf, w, cs, sbuf, rx, zbuf, rz, obuf, ybuf, ry, rmm,
    grid_sem, leg_sem, xs_sem, xr_sem, zs_sem, zr_sem, ys_sem, yr_sem, ms_sem, mr_sem,
):
    ew, ns = lax.axis_index("ew"), lax.axis_index("ns")
    x, z = lax.rem(ew, NX), lax.div(ew, NX)
    rows = gridv.shape[2]
    points = gridv.shape[3]
    chunks = rows // CH

    grid_copy = pltpu.make_async_copy(grid_hbm, gridv, grid_sem)
    grid_copy.start()
    leg_copies = [
        pltpu.make_async_copy(leg_hbm.at[:, 0, k * 128 : (k + 1) * 128], legv.at[k], leg_sem.at[k])
        for k in range(legv.shape[0])
    ]
    for copy in leg_copies:
        copy.start()

    barrier = pltpu.get_barrier_semaphore()
    for d in range(1, NX):
        pl.semaphore_signal(barrier, inc=1, device_id={"ew": z * NX + lax.rem(x + d, NX)}, device_id_type=MESH)
    for d in range(1, NZ):
        pl.semaphore_signal(barrier, inc=1, device_id={"ew": lax.rem(z + d, NZ) * NX + x}, device_id_type=MESH)
    for d in range(1, NS):
        pl.semaphore_signal(barrier, inc=1, device_id={"ns": lax.rem(ns + d, NS)}, device_id_type=MESH)

    w[...] = jnp.zeros_like(w)
    xf[...] = jnp.zeros_like(xf)

    lane = lax.broadcasted_iota(jnp.int32, (16, 128), 1)
    sub16 = lax.broadcasted_iota(jnp.int32, (16, 128), 0)
    pair_of = (lane & 63) >> 2
    wave = jnp.zeros((16, 128), jnp.int32)
    for p in range(16):
        wave = jnp.where(pair_of == p, waves_s[p], wave)
    wave = jnp.where((lane & 2) == 0, wave, truncation - wave).astype(F32)
    imaginary = (lane & 1) == 1
    low_half = lane < 64
    first = ew * points
    product_a = wave * (first + 16 * sub16).astype(F32)
    product_b = wave * sub16.astype(F32)
    point0 = (first + sub16).astype(F32)
    point_end = (first + points).astype(F32)

    grid_copy.wait()

    def chunk(c, _):
        def convert(zz, _):
            for xx in range(NX):
                field = order_s[zz * NX + xx]
                for h in range(2):
                    at = pl.multiple_of((h * 32 + xx * NZ + zz) * CH, CH)
                    block = gridv[field, h, pl.ds(pl.multiple_of(c * CH, CH), CH), :].astype(F32)
                    xf[0, pl.ds(at, CH), :] = block[:, 0:128]
                    xf[1, pl.ds(at, CH), 0 : points - 128] = block[:, 128:points]
            return 0

        lax.fori_loop(0, NZ, convert, 0)

        def half(g, _):
            for j in range(4):
                row0 = g * 8 + j
                band0 = band_s[ns * rows + c * CH + row0]
                band1 = band_s[ns * rows + c * CH + row0 + 4]
                length = jnp.where(low_half, 20 + 4 * band0, 20 + 4 * band1).astype(F32)
                inverse = 1.0 / length
                cos_a, sin_a = _cos_sin(product_a, length, inverse)
                cos_b, sin_b = _cos_sin(product_b, length, inverse)
                cs[j, 0] = jnp.where(imaginary, -sin_a, cos_a) * inverse
                cs[j, 1] = jnp.where(imaginary, cos_a, sin_a) * inverse
                end = jnp.minimum(length, point_end) - point0
                for a in range(11):
                    value = cs[j, 0, a : a + 1, :] * cos_b - cs[j, 1, a : a + 1, :] * sin_b
                    value = jnp.where(end > 16.0 * a, value, 0.0)
                    high = value.astype(BF16)
                    low = (value - high.astype(F32)).astype(BF16)
                    w[j, 16 * a : 16 * a + 16, 0:128] = high
                    w[j, 16 * a : 16 * a + 16, 128:256] = low
                sides = []
                for side in range(2):
                    x0 = xf[side, pl.ds(row0, 64, stride=CH), :].astype(BF16)
                    x1 = xf[side, pl.ds(row0 + 4, 64, stride=CH), :].astype(BF16)
                    sides.append(jnp.concatenate([x0, x1], 0))
                both = jnp.dot(jnp.concatenate(sides, 1), w[j], preferred_element_type=F32)
                both = both[:, :128] + both[:, 128:]
                out = jnp.where(lax.broadcasted_iota(jnp.int32, (64, 128), 1) < 64, both[:64], both[64:])
                for h in range(2):
                    for xx in range(NX):
                        sbuf[c, xx, pl.ds(g * 8 + h * 4 + j, NZ, stride=CH), :] = out[h * 32 + xx * NZ : h * 32 + xx * NZ + NZ]
            return 0

        lax.fori_loop(0, CH // 8, half, 0)

        @pl.when(c == 0)
        def _():
            pl.semaphore_wait(barrier, NX - 1 + NZ - 1 + NS - 1)

        for d in range(1, NX):
            x_copy(c, d).start()
        return 0

    def x_copy(c, d):
        to = lax.rem(x + d, NX)
        return pltpu.make_async_remote_copy(
            src_ref=sbuf.at[c, to], dst_ref=rx.at[c, d - 1],
            send_sem=xs_sem.at[c, d - 1], recv_sem=xr_sem.at[c, d - 1],
            device_id={"ew": z * NX + to}, device_id_type=MESH)

    def z_copy(c, d):
        to = lax.rem(z + d, NZ)
        return pltpu.make_async_remote_copy(
            src_ref=zbuf.at[c, pl.ds(pl.multiple_of(to * CH, CH), CH)], dst_ref=rz.at[c, d - 1],
            send_sem=zs_sem.at[c, d - 1], recv_sem=zr_sem.at[c, d - 1],
            device_id={"ew": to * NX + x}, device_id_type=MESH)

    def y_copy(d):
        to = lax.rem(ns + d, NS)
        return pltpu.make_async_remote_copy(
            src_ref=ybuf.at[to], dst_ref=ry.at[ns],
            send_sem=ys_sem.at[d - 1], recv_sem=yr_sem.at[d - 1],
            device_id={"ns": to}, device_id_type=MESH)

    def m_copy(d):
        to = lax.rem(ns + d, NS)
        return pltpu.make_async_remote_copy(
            src_ref=rmm.at[0], dst_ref=rmm.at[d],
            send_sem=ms_sem.at[d - 1], recv_sem=mr_sem.at[d - 1],
            device_id={"ns": to}, device_id_type=MESH)

    lax.fori_loop(0, chunks, chunk, 0)

    for copy in leg_copies:
        copy.wait()

    def split(i, _):
        at = pl.ds(pl.multiple_of(i * 128, 128), 128)
        value = legv[i].T
        high = value.astype(BF16)
        leghi[at, :] = high
        leglo[at, :] = (value - high.astype(F32)).astype(BF16)
        return 0

    lax.fori_loop(0, legv.shape[0], split, 0)

    def second(c, _):
        for d in range(1, NX):
            x_copy(c, d).wait_recv()
        zbuf[c] = sbuf[c, x] + rx[c, 0] + rx[c, 1] + rx[c, 2]
        for d in range(1, NZ):
            z_copy(c, d).start()
        return 0

    lax.fori_loop(0, chunks, second, 0)

    sub8 = lax.broadcasted_iota(jnp.int32, (8, 128), 0)
    lane8 = lax.broadcasted_iota(jnp.int32, (8, 128), 1)
    obuf[...] = jnp.zeros_like(obuf)

    def third(c, _):
        for d in range(1, NZ):
            z_copy(c, d).wait_recv()
        total = zbuf[c, pl.ds(pl.multiple_of(z * CH, CH), CH)]
        for d in range(NZ - 1):
            total = total + rz[c, d]
        for g in range(CH // 8):
            o = total[g * 8 : g * 8 + 8]
            r = pltpu.roll(o, 4, 0)
            o = jnp.where(sub8 < 4, o + r, r - o)
            r = pltpu.roll(pltpu.roll(o, 4, 0), 64, 1)
            o = jnp.where((sub8 < 4) == (lane8 < 64), o, r)
            obuf[pl.ds(pl.multiple_of(c * CH + g * 8, 8), 8), :] = o
        return 0

    lax.fori_loop(0, chunks, third, 0)

    turned = obuf[...].T
    for p in range(NS):
        ybuf[p] = jnp.concatenate([turned[4 * p : 4 * p + 4], turned[64 + 4 * p : 68 + 4 * p]], 0)
    for d in range(1, NS):
        y_copy(d).start()
    ry[ns] = ybuf[ns]

    columns = leghi.shape[1]
    column = lax.broadcasted_iota(jnp.int32, (2, columns), 1)
    wavenum = waves_s[ns]
    in_first = column <= truncation - wavenum
    shifted = jnp.where(in_first, column, column - (truncation - wavenum + 1))
    even = (shifted & 1) == 0
    degree = jnp.where(in_first, wavenum + column, column - 1).astype(F32)
    field_type = lax.div(order_s[ew], levels)
    power, bits = power_s[0], bits_s[0]
    for t in range(1, bits_s.shape[0]):
        power = jnp.where(field_type == t, power_s[t], power)
        bits = jnp.where(field_type == t, bits_s[t], bits)
    weight = jnp.exp(power * jnp.log(degree * (degree + 1.0) + 2.0))
    spread = (lax.shift_left(jnp.int32(1), bits) - 1).astype(F32) * (1.0 / 4096.0)

    for d in range(1, NS):
        y_copy(d).wait_recv()
    pieces = [None] * (rows * NS // 128)
    for i in range(NS):
        at, off = divmod(i * rows, 128)
        value = ry[i] if off == 0 else pltpu.roll(ry[i], off, 1)
        if off + rows <= 128:
            parts = [(at, value)]
        else:
            parts = [(at, jnp.where(lane8 >= off, value, 0.0)), (at + 1, jnp.where(lane8 < off, value, 0.0))]
        for k, v in parts:
            pieces[k] = v if pieces[k] is None else pieces[k] + v
    stacked = jnp.concatenate(pieces, 1)
    high = stacked.astype(BF16).astype(F32)
    both = jnp.concatenate([high, stacked - high], 0).astype(BF16)
    by_high = jnp.dot(both, leghi[...], preferred_element_type=F32)
    by_low = jnp.dot(both, leglo[...], preferred_element_type=F32)
    result = by_high[:8] + by_high[8:] + by_low[:8]

    chosen = jnp.where(
        in_first,
        jnp.where(even, result[0:2], result[4:6]),
        jnp.where(even, result[2:4], result[6:8]),
    )
    scaled = chosen * weight
    most = jnp.max(scaled)
    least = jnp.min(scaled)
    rmm[0] = jnp.where(lane8 < 64, most, -least)
    for d in range(1, NS):
        m_copy(d).start()
    for d in range(1, NS):
        m_copy(d).wait_recv()
    top = rmm[0]
    for d in range(1, NS):
        top = jnp.maximum(top, rmm[d])
    highest = jnp.max(jnp.where(lane8 < 64, top, -jnp.inf))
    lowest = -jnp.max(jnp.where(lane8 < 64, -jnp.inf, top))
    span = highest - lowest + 1e-6
    out_ref[0, 0] = (scaled - lowest) / span * spread

    def sent(c, _):
        for d in range(1, NX):
            x_copy(c, d).wait_send()
        for d in range(1, NZ):
            z_copy(c, d).wait_send()
        return 0

    lax.fori_loop(0, chunks, sent, 0)
    for d in range(1, NS):
        y_copy(d).wait_send()
        m_copy(d).wait_send()


def shards(grid, band_rows, wave_pairs, packer_order, field_bits, field_power, legendre):
    fields, hemis, rows, points = grid.shape
    lats, columns = legendre.shape[1:]
    truncation = columns - 2
    levels = fields // field_bits.shape[0]
    chunks = rows // CH
    smem = pl.BlockSpec(memory_space=pltpu.SMEM)
    hbm = pl.BlockSpec(memory_space=pltpu.HBM)
    dma = pltpu.SemaphoreType.DMA
    return pl.pallas_call(
        functools.partial(kernel, truncation, levels),
        out_shape=jax.ShapeDtypeStruct((1, 1, 2, columns), F32),
        in_specs=[smem] * 5 + [hbm] * 2,
        out_specs=pl.BlockSpec(memory_space=pltpu.VMEM),
        scratch_shapes=[
            pltpu.VMEM((fields, hemis, rows, points), BF16),
            pltpu.VMEM((lats // 128, columns, 128), F32),
            pltpu.VMEM((lats, columns), BF16),
            pltpu.VMEM((lats, columns), BF16),
            pltpu.VMEM((2, fields * hemis * CH, 128), F32),
            pltpu.VMEM((4, 256, 256), BF16),
            pltpu.VMEM((4, 2, 16, 128), F32),
            pltpu.VMEM((chunks, NX, NZ * CH, 128), F32),
            pltpu.VMEM((chunks, NX - 1, NZ * CH, 128), F32),
            pltpu.VMEM((chunks, NZ * CH, 128), F32),
            pltpu.VMEM((chunks, NZ - 1, CH, 128), F32),
            pltpu.VMEM((128, 128), F32),
            pltpu.VMEM((NS, 8, 128), F32),
            pltpu.VMEM((NS, 8, 128), F32),
            pltpu.VMEM((NS, 8, 128), F32),
            dma,
            dma((lats // 128,)),
            dma((chunks, NX - 1)),
            dma((chunks, NX - 1)),
            dma((chunks, NZ - 1)),
            dma((chunks, NZ - 1)),
            dma((NS - 1,)),
            dma((NS - 1,)),
            dma((NS - 1,)),
            dma((NS - 1,)),
        ],
        compiler_params=pltpu.CompilerParams(
            collective_id=0, has_side_effects=True, vmem_limit_bytes=61 * 2**20
        ),
    )(band_rows, wave_pairs, packer_order, field_bits, field_power, grid, jnp.transpose(legendre, (2, 0, 1)))


def solution(mesh):
    return jax.shard_map(
        shards,
        mesh=mesh,
        in_specs=(P(None, None, "ns", "ew"), P(), P(), P(), P(), P(), P("ns", None, None)),
        out_specs=P("ew", "ns", None, None),
        check_vma=False,
    )
```

```python
import functools

import jax
import jax.numpy as jnp
import numpy as np
from jax import lax
from jax.experimental import pallas as pl
from jax.experimental.pallas import tpu as pltpu
from jax.sharding import PartitionSpec as P

MESH = pl.DeviceIdType.MESH
NX = 4
NZ = 8
NS = 16
CH = 16
HALF = NZ * CH // 2
F32 = jnp.float32
BF16 = jnp.bfloat16


def _fit(function, terms):
    z = 0.125 + 0.125 * np.cos(np.pi * (np.arange(200) + 0.5) / 200)
    cheb = np.polynomial.chebyshev.Chebyshev.fit(z, function(np.sqrt(z)), terms - 1, domain=[0, 0.25])
    return [float(v) for v in cheb.convert(kind=np.polynomial.Polynomial).coef]


COS = _fit(lambda t: np.cos(2 * np.pi * t), 8)
SIN = _fit(lambda t: np.sin(2 * np.pi * t) / t, 8)


def _horner(coefs, z):
    total = jnp.full_like(z, coefs[-1])
    for c in coefs[-2::-1]:
        total = total * z + c
    return total


def _cos_sin(product, length, inverse):
    rest = product - jnp.round(product * inverse) * length
    t = rest * inverse
    z = t * t
    return _horner(COS, z), t * _horner(SIN, z)


def kernel(
    truncation, levels,
    band_s, waves_s, order_s, bits_s, power_s, grid_hbm, leg_hbm,
    out_ref,
    gridv, legv, leghi, leglo, xf, w, cs, sbuf, rfar, rx, zbuf, rz, obuf, ybuf, ry, rmm,
    grid_sem, leg_sem, fs_sem, fr_sem, xs_sem, xr_sem, zs_sem, zr_sem, ys_sem, yr_sem, ms_sem, mr_sem,
):
    ew, ns = lax.axis_index("ew"), lax.axis_index("ns")
    x, z = lax.rem(ew, NX), lax.div(ew, NX)
    rows = gridv.shape[2]
    points = gridv.shape[3]
    chunks = rows // CH

    grid_copy = pltpu.make_async_copy(grid_hbm, gridv, grid_sem)
    grid_copy.start()
    leg_copies = [
        pltpu.make_async_copy(leg_hbm.at[:, 0, k * 128 : (k + 1) * 128], legv.at[k], leg_sem.at[k])
        for k in range(legv.shape[0])
    ]
    for copy in leg_copies:
        copy.start()

    barrier = pltpu.get_barrier_semaphore()
    for d in range(1, NX):
        pl.semaphore_signal(barrier, inc=1, device_id={"ew": z * NX + lax.rem(x + d, NX)}, device_id_type=MESH)
    for d in range(1, NZ):
        pl.semaphore_signal(barrier, inc=1, device_id={"ew": lax.rem(z + d, NZ) * NX + x}, device_id_type=MESH)
    for d in range(1, NS):
        pl.semaphore_signal(barrier, inc=1, device_id={"ns": lax.rem(ns + d, NS)}, device_id_type=MESH)

    w[...] = jnp.zeros_like(w)
    xf[1] = jnp.zeros_like(xf[1])

    lane = lax.broadcasted_iota(jnp.int32, (16, 128), 1)
    sub16 = lax.broadcasted_iota(jnp.int32, (16, 128), 0)
    pair_of = (lane & 63) >> 2
    wave = jnp.zeros((16, 128), jnp.int32)
    for p in range(16):
        wave = jnp.where(pair_of == p, waves_s[p], wave)
    wave = jnp.where((lane & 2) == 0, wave, truncation - wave).astype(F32)
    imaginary = (lane & 1) == 1
    low_half = lane < 64
    first = ew * points
    product_a = wave * (first + 16 * sub16).astype(F32)
    product_b = wave * sub16.astype(F32)
    point0 = (first + sub16).astype(F32)
    point_end = (first + points).astype(F32)

    grid_copy.wait()

    def neighbour(side):
        return lax.rem(x + (1 if side == 0 else NX - 1), NX)

    def far_copy(c, side):
        return pltpu.make_async_remote_copy(
            src_ref=sbuf.at[c, lax.rem(x + 2, NX), pl.ds(side * HALF, HALF)], dst_ref=rfar.at[c, side],
            send_sem=fs_sem.at[c, side], recv_sem=fr_sem.at[c, side],
            device_id={"ew": z * NX + neighbour(side)}, device_id_type=MESH)

    def near_copy(c, side, part):
        rows = pl.ds(part * HALF, HALF)
        return pltpu.make_async_remote_copy(
            src_ref=sbuf.at[c, neighbour(side), rows], dst_ref=rx.at[c, side, rows],
            send_sem=xs_sem.at[c, side, part], recv_sem=xr_sem.at[c, side, part],
            device_id={"ew": z * NX + neighbour(side)}, device_id_type=MESH)

    def z_copy(c, d):
        to = lax.rem(z + d, NZ)
        return pltpu.make_async_remote_copy(
            src_ref=zbuf.at[c, pl.ds(pl.multiple_of(to * CH, CH), CH)], dst_ref=rz.at[c, d - 1],
            send_sem=zs_sem.at[c, d - 1], recv_sem=zr_sem.at[c, d - 1],
            device_id={"ew": to * NX + x}, device_id_type=MESH)

    def y_copy(d):
        to = lax.rem(ns + d, NS)
        return pltpu.make_async_remote_copy(
            src_ref=ybuf.at[to], dst_ref=ry.at[ns],
            send_sem=ys_sem.at[d - 1], recv_sem=yr_sem.at[d - 1],
            device_id={"ns": to}, device_id_type=MESH)

    def m_copy(d):
        to = lax.rem(ns + d, NS)
        return pltpu.make_async_remote_copy(
            src_ref=rmm.at[0, 0:1], dst_ref=rmm.at[d, 0:1],
            send_sem=ms_sem.at[d - 1], recv_sem=mr_sem.at[d - 1],
            device_id={"ns": to}, device_id_type=MESH)

    def pass_on(c):
        for side in (0, 1):
            far_copy(c, side).wait_recv()
            rows = pl.ds(side * HALF, HALF)
            sbuf[c, neighbour(side), rows] = sbuf[c, neighbour(side), rows] + rfar[c, side]
            near_copy(c, side, side).start()

    def along_z(c):
        for side in (0, 1):
            for part in (0, 1):
                near_copy(c, side, part).wait_recv()
        zbuf[c] = sbuf[c, x] + rx[c, 0] + rx[c, 1]
        for d in range(1, NZ):
            z_copy(c, d).start()

    def chunk(c, _):
        def convert(zz, _):
            for xx in range(NX):
                field = order_s[zz * NX + xx]
                for h in range(2):
                    at = pl.multiple_of((h * 32 + xx * NZ + zz) * CH, CH)
                    block = gridv[field, h, pl.ds(pl.multiple_of(c * CH, CH), CH), :].astype(F32)
                    xf[0, pl.ds(at, CH), :] = block[:, 0:128]
                    xf[1, pl.ds(at, CH), 0 : points - 128] = block[:, 128:points]
            return 0

        lax.fori_loop(0, NZ, convert, 0)

        def half(g, _):
            for j in range(4):
                row0 = g * 8 + j
                band0 = band_s[ns * rows + c * CH + row0]
                band1 = band_s[ns * rows + c * CH + row0 + 4]
                length = jnp.where(low_half, 20 + 4 * band0, 20 + 4 * band1).astype(F32)
                inverse = 1.0 / length
                cos_a, sin_a = _cos_sin(product_a, length, inverse)
                cos_b, sin_b = _cos_sin(product_b, length, inverse)
                cs[j, 0] = jnp.where(imaginary, -sin_a, cos_a) * inverse
                cs[j, 1] = jnp.where(imaginary, cos_a, sin_a) * inverse
                end = jnp.minimum(length, point_end) - point0
                for a in range(11):
                    value = cs[j, 0, a : a + 1, :] * cos_b - cs[j, 1, a : a + 1, :] * sin_b
                    value = jnp.where(end > 16.0 * a, value, 0.0)
                    high = value.astype(BF16)
                    low = (value - high.astype(F32)).astype(BF16)
                    w[j, 16 * a : 16 * a + 16, 0:128] = high
                    w[j, 16 * a : 16 * a + 16, 128:256] = low
                sides = []
                for side in range(2):
                    x0 = xf[side, pl.ds(row0, 64, stride=CH), :].astype(BF16)
                    x1 = xf[side, pl.ds(row0 + 4, 64, stride=CH), :].astype(BF16)
                    sides.append(jnp.concatenate([x0, x1], 0))
                both = jnp.dot(jnp.concatenate(sides, 1), w[j], preferred_element_type=F32)
                both = both[:, :128] + both[:, 128:]
                out = jnp.where(lax.broadcasted_iota(jnp.int32, (64, 128), 1) < 64, both[:64], both[64:])
                for h in range(2):
                    for xx in range(NX):
                        sbuf[c, xx, pl.ds(g * 8 + h * 4 + j, NZ, stride=CH), :] = out[h * 32 + xx * NZ : h * 32 + xx * NZ + NZ]
            return 0

        lax.fori_loop(0, CH // 8, half, 0)

        @pl.when(c == 0)
        def _():
            pl.semaphore_wait(barrier, NX - 1 + NZ - 1 + NS - 1)

        for side in (0, 1):
            far_copy(c, side).start()
            near_copy(c, side, 1 - side).start()

        @pl.when(c >= 2)
        def _():
            pass_on(c - 2)

        return 0

    lax.fori_loop(0, chunks, chunk, 0)

    pass_on(chunks - 2)
    along_z(0)
    pass_on(chunks - 1)

    def second(c, _):
        along_z(c)
        return 0

    lax.fori_loop(1, chunks, second, 0)

    for copy in leg_copies:
        copy.wait()

    def split(i, _):
        at = pl.ds(pl.multiple_of(i * 128, 128), 128)
        value = legv[i].T
        high = value.astype(BF16)
        leghi[at, :] = high
        leglo[at, :] = (value - high.astype(F32)).astype(BF16)
        return 0

    lax.fori_loop(0, legv.shape[0], split, 0)

    sub8 = lax.broadcasted_iota(jnp.int32, (8, 128), 0)
    lane8 = lax.broadcasted_iota(jnp.int32, (8, 128), 1)
    obuf[...] = jnp.zeros_like(obuf)

    def third(c, _):
        for d in range(1, NZ):
            z_copy(c, d).wait_recv()
        total = zbuf[c, pl.ds(pl.multiple_of(z * CH, CH), CH)]
        for d in range(NZ - 1):
            total = total + rz[c, d]
        for g in range(CH // 8):
            o = total[g * 8 : g * 8 + 8]
            r = pltpu.roll(o, 4, 0)
            o = jnp.where(sub8 < 4, o + r, r - o)
            r = pltpu.roll(pltpu.roll(o, 4, 0), 64, 1)
            o = jnp.where((sub8 < 4) == (lane8 < 64), o, r)
            obuf[pl.ds(pl.multiple_of(c * CH + g * 8, 8), 8), :] = o
        return 0

    lax.fori_loop(0, chunks, third, 0)

    turned = obuf[...].T
    for p in range(NS):
        ybuf[p] = jnp.concatenate([turned[4 * p : 4 * p + 4], turned[64 + 4 * p : 68 + 4 * p]], 0)
    for d in range(1, NS):
        y_copy(d).start()
    ry[ns] = ybuf[ns]

    columns = leghi.shape[1]
    column = lax.broadcasted_iota(jnp.int32, (2, columns), 1)
    wavenum = waves_s[ns]
    in_first = column <= truncation - wavenum
    shifted = jnp.where(in_first, column, column - (truncation - wavenum + 1))
    even = (shifted & 1) == 0
    degree = jnp.where(in_first, wavenum + column, column - 1).astype(F32)
    field_type = lax.div(order_s[ew], levels)
    power, bits = power_s[0], bits_s[0]
    for t in range(1, bits_s.shape[0]):
        power = jnp.where(field_type == t, power_s[t], power)
        bits = jnp.where(field_type == t, bits_s[t], bits)
    weight = jnp.exp(power * jnp.log(degree * (degree + 1.0) + 2.0))
    spread = (lax.shift_left(jnp.int32(1), bits) - 1).astype(F32) * (1.0 / 4096.0)

    for d in range(1, NS):
        y_copy(d).wait_recv()
    pieces = [None] * (rows * NS // 128)
    for i in range(NS):
        at, off = divmod(i * rows, 128)
        value = ry[i] if off == 0 else pltpu.roll(ry[i], off, 1)
        if off + rows <= 128:
            parts = [(at, value)]
        else:
            parts = [(at, jnp.where(lane8 >= off, value, 0.0)), (at + 1, jnp.where(lane8 < off, value, 0.0))]
        for k, v in parts:
            pieces[k] = v if pieces[k] is None else pieces[k] + v
    stacked = jnp.concatenate(pieces, 1)
    high = stacked.astype(BF16).astype(F32)
    both = jnp.concatenate([high, stacked - high], 0).astype(BF16)
    by_high = jnp.dot(both, leghi[...], preferred_element_type=F32)
    by_low = jnp.dot(both, leglo[...], preferred_element_type=F32)
    result = by_high[:8] + by_high[8:] + by_low[:8]

    chosen = jnp.where(
        in_first,
        jnp.where(even, result[0:2], result[4:6]),
        jnp.where(even, result[2:4], result[6:8]),
    )
    scaled = chosen * weight
    most = jnp.max(jnp.max(scaled, axis=0, keepdims=True), axis=1, keepdims=True)
    least = jnp.min(jnp.min(scaled, axis=0, keepdims=True), axis=1, keepdims=True)
    rmm[0, 0:1] = jnp.where(lane8[0:1] < 64, most, -least)
    for d in range(1, NS):
        m_copy(d).start()
    for d in range(1, NS):
        m_copy(d).wait_recv()
    top = rmm[0, 0:1]
    for d in range(1, NS):
        top = jnp.maximum(top, rmm[d, 0:1])
    highest = top[:, 0:1]
    lowest = -top[:, 64:65]
    span = highest - lowest + 1e-6
    out_ref[0, 0] = (scaled - lowest) / span * spread

    def sent(c, _):
        for side in (0, 1):
            far_copy(c, side).wait_send()
            for part in (0, 1):
                near_copy(c, side, part).wait_send()
        for d in range(1, NZ):
            z_copy(c, d).wait_send()
        return 0

    lax.fori_loop(0, chunks, sent, 0)
    for d in range(1, NS):
        y_copy(d).wait_send()
        m_copy(d).wait_send()


def shards(grid, band_rows, wave_pairs, packer_order, field_bits, field_power, legendre):
    fields, hemis, rows, points = grid.shape
    lats, columns = legendre.shape[1:]
    truncation = columns - 2
    levels = fields // field_bits.shape[0]
    chunks = rows // CH
    smem = pl.BlockSpec(memory_space=pltpu.SMEM)
    hbm = pl.BlockSpec(memory_space=pltpu.HBM)
    dma = pltpu.SemaphoreType.DMA
    return pl.pallas_call(
        functools.partial(kernel, truncation, levels),
        out_shape=jax.ShapeDtypeStruct((1, 1, 2, columns), F32),
        in_specs=[smem] * 5 + [hbm] * 2,
        out_specs=pl.BlockSpec(memory_space=pltpu.VMEM),
        scratch_shapes=[
            pltpu.VMEM((fields, hemis, rows, points), BF16),
            pltpu.VMEM((lats // 128, columns, 128), F32),
            pltpu.VMEM((lats, columns), BF16),
            pltpu.VMEM((lats, columns), BF16),
            pltpu.VMEM((2, fields * hemis * CH, 128), F32),
            pltpu.VMEM((4, 256, 256), BF16),
            pltpu.VMEM((4, 2, 16, 128), F32),
            pltpu.VMEM((chunks, NX, NZ * CH, 128), F32),
            pltpu.VMEM((chunks, 2, HALF, 128), F32),
            pltpu.VMEM((chunks, 2, NZ * CH, 128), F32),
            pltpu.VMEM((chunks, NZ * CH, 128), F32),
            pltpu.VMEM((chunks, NZ - 1, CH, 128), F32),
            pltpu.VMEM((128, 128), F32),
            pltpu.VMEM((NS, 8, 128), F32),
            pltpu.VMEM((NS, 8, 128), F32),
            pltpu.VMEM((NS, 8, 128), F32),
            dma,
            dma((lats // 128,)),
            dma((chunks, 2)),
            dma((chunks, 2)),
            dma((chunks, 2, 2)),
            dma((chunks, 2, 2)),
            dma((chunks, NZ - 1)),
            dma((chunks, NZ - 1)),
            dma((NS - 1,)),
            dma((NS - 1,)),
            dma((NS - 1,)),
            dma((NS - 1,)),
        ],
        compiler_params=pltpu.CompilerParams(
            collective_id=0, has_side_effects=True, vmem_limit_bytes=61 * 2**20
        ),
    )(band_rows, wave_pairs, packer_order, field_bits, field_power, grid, jnp.transpose(legendre, (2, 0, 1)))


def solution(mesh):
    return jax.shard_map(
        shards,
        mesh=mesh,
        in_specs=(P(None, None, "ns", "ew"), P(), P(), P(), P(), P(), P("ns", None, None)),
        out_specs=P("ew", "ns", None, None),
        check_vma=False,
    )
```

```python
import functools

import jax
import jax.numpy as jnp
import numpy as np
from jax import lax
from jax.experimental import pallas as pl
from jax.experimental.pallas import tpu as pltpu
from jax.sharding import PartitionSpec as P

MESH = pl.DeviceIdType.MESH
NX = 4
NZ = 8
NS = 16
CH = 16
HALF = NZ * CH // 2
F32 = jnp.float32
BF16 = jnp.bfloat16


def _fit(function, terms):
    z = 0.125 + 0.125 * np.cos(np.pi * (np.arange(200) + 0.5) / 200)
    cheb = np.polynomial.chebyshev.Chebyshev.fit(z, function(np.sqrt(z)), terms - 1, domain=[0, 0.25])
    return [float(v) for v in cheb.convert(kind=np.polynomial.Polynomial).coef]


COS = _fit(lambda t: np.cos(2 * np.pi * t), 8)
SIN = _fit(lambda t: np.sin(2 * np.pi * t) / t, 8)


def _horner(coefs, z):
    total = jnp.full_like(z, coefs[-1])
    for c in coefs[-2::-1]:
        total = total * z + c
    return total


def _cos_sin(product, length, inverse):
    rest = product - jnp.round(product * inverse) * length
    t = rest * inverse
    z = t * t
    return _horner(COS, z), t * _horner(SIN, z)


def kernel(
    truncation, levels,
    band_s, waves_s, order_s, bits_s, power_s, grid_hbm, leg_hbm,
    out_ref,
    gridv0, gridv, legv, leghi, leglo, xf, w, cs, sbuf, rfar, rx, zbuf, rz, rz0, sum0, rx0, obuf, ybuf, ry, rmm,
    grid_sem, leg_sem, fs_sem, fr_sem, xs_sem, xr_sem, x0s_sem, x0r_sem, zs_sem, zr_sem, ys_sem, yr_sem, ms_sem, mr_sem,
):
    ew, ns = lax.axis_index("ew"), lax.axis_index("ns")
    x, z = lax.rem(ew, NX), lax.div(ew, NX)
    rows, points = grid_hbm.shape[2:]
    chunks = rows // CH

    grid_copy0 = pltpu.make_async_copy(grid_hbm.at[:, :, 0:CH], gridv0, grid_sem.at[0])
    grid_copy0.start()
    grid_copy = pltpu.make_async_copy(grid_hbm.at[:, :, CH:rows], gridv, grid_sem.at[1])
    grid_copy.start()
    leg_copies = [
        pltpu.make_async_copy(leg_hbm.at[:, 0, k * 128 : (k + 1) * 128], legv.at[k], leg_sem.at[k])
        for k in range(legv.shape[0])
    ]
    for copy in leg_copies:
        copy.start()

    barrier = pltpu.get_barrier_semaphore()
    for d in range(1, NX):
        pl.semaphore_signal(barrier, inc=1, device_id={"ew": z * NX + lax.rem(x + d, NX)}, device_id_type=MESH)
    for d in range(1, NZ):
        pl.semaphore_signal(barrier, inc=1, device_id={"ew": lax.rem(z + d, NZ) * NX + x}, device_id_type=MESH)
    for d in range(1, NS):
        pl.semaphore_signal(barrier, inc=1, device_id={"ns": lax.rem(ns + d, NS)}, device_id_type=MESH)

    w[...] = jnp.zeros_like(w)
    xf[1] = jnp.zeros_like(xf[1])

    lane = lax.broadcasted_iota(jnp.int32, (16, 128), 1)
    sub16 = lax.broadcasted_iota(jnp.int32, (16, 128), 0)
    pair_of = (lane & 63) >> 2
    wave = jnp.zeros((16, 128), jnp.int32)
    for p in range(16):
        wave = jnp.where(pair_of == p, waves_s[p], wave)
    wave = jnp.where((lane & 2) == 0, wave, truncation - wave).astype(F32)
    imaginary = (lane & 1) == 1
    low_half = lane < 64
    first = ew * points
    product_a = wave * (first + 16 * sub16).astype(F32)
    product_b = wave * sub16.astype(F32)
    point0 = (first + sub16).astype(F32)
    point_end = (first + points).astype(F32)

    def neighbour(side):
        return lax.rem(x + (1 if side == 0 else NX - 1), NX)

    def far_copy(c, side):
        return pltpu.make_async_remote_copy(
            src_ref=sbuf.at[c, lax.rem(x + 2, NX), pl.ds(side * HALF, HALF)], dst_ref=rfar.at[c, side],
            send_sem=fs_sem.at[c, side], recv_sem=fr_sem.at[c, side],
            device_id={"ew": z * NX + neighbour(side)}, device_id_type=MESH)

    def near_copy(c, side, part):
        rows = pl.ds(part * HALF, HALF)
        return pltpu.make_async_remote_copy(
            src_ref=sbuf.at[c, neighbour(side), rows], dst_ref=rx.at[c, side, rows],
            send_sem=xs_sem.at[c, side, part], recv_sem=xr_sem.at[c, side, part],
            device_id={"ew": z * NX + neighbour(side)}, device_id_type=MESH)

    def z_copy(c, d):
        to = lax.rem(z + d, NZ)
        return pltpu.make_async_remote_copy(
            src_ref=zbuf.at[c, pl.ds(pl.multiple_of(to * CH, CH), CH)], dst_ref=rz.at[c, d - 1],
            send_sem=zs_sem.at[c, d - 1], recv_sem=zr_sem.at[c, d - 1],
            device_id={"ew": to * NX + x}, device_id_type=MESH)

    def y_copy(d):
        to = lax.rem(ns + d, NS)
        return pltpu.make_async_remote_copy(
            src_ref=ybuf.at[to], dst_ref=ry.at[ns],
            send_sem=ys_sem.at[d - 1], recv_sem=yr_sem.at[d - 1],
            device_id={"ns": to}, device_id_type=MESH)

    def m_copy(d):
        to = lax.rem(ns + d, NS)
        return pltpu.make_async_remote_copy(
            src_ref=rmm.at[0, 0:1], dst_ref=rmm.at[d, 0:1],
            send_sem=ms_sem.at[d - 1], recv_sem=mr_sem.at[d - 1],
            device_id={"ns": to}, device_id_type=MESH)

    def pass_on(c):
        for side in (0, 1):
            far_copy(c, side).wait_recv()
            rows = pl.ds(side * HALF, HALF)
            sbuf[c, neighbour(side), rows] = sbuf[c, neighbour(side), rows] + rfar[c, side]
            near_copy(c, side, side).start()

    def along_z(c):
        for side in (0, 1):
            for part in (0, 1):
                near_copy(c, side, part).wait_recv()
        zbuf[c] = sbuf[c, x] + rx[c, 0] + rx[c, 1]
        for d in range(1, NZ):
            z_copy(c, d).start()

    def compute(c, grid_ref, grid_row):
        def convert(zz, _):
            for xx in range(NX):
                field = order_s[zz * NX + xx]
                for h in range(2):
                    at = pl.multiple_of((h * 32 + xx * NZ + zz) * CH, CH)
                    block = grid_ref[field, h, pl.ds(grid_row, CH), :].astype(F32)
                    xf[0, pl.ds(at, CH), :] = block[:, 0:128]
                    xf[1, pl.ds(at, CH), 0 : points - 128] = block[:, 128:points]
            return 0

        lax.fori_loop(0, NZ, convert, 0)

        def half(g, _):
            for j in range(4):
                row0 = g * 8 + j
                band0 = band_s[ns * rows + c * CH + row0]
                band1 = band_s[ns * rows + c * CH + row0 + 4]
                length = jnp.where(low_half, 20 + 4 * band0, 20 + 4 * band1).astype(F32)
                inverse = 1.0 / length
                cos_a, sin_a = _cos_sin(product_a, length, inverse)
                cos_b, sin_b = _cos_sin(product_b, length, inverse)
                cs[j, 0] = jnp.where(imaginary, -sin_a, cos_a) * inverse
                cs[j, 1] = jnp.where(imaginary, cos_a, sin_a) * inverse
                end = jnp.minimum(length, point_end) - point0
                for a in range(11):
                    value = cs[j, 0, a : a + 1, :] * cos_b - cs[j, 1, a : a + 1, :] * sin_b
                    value = jnp.where(end > 16.0 * a, value, 0.0)
                    high = value.astype(BF16)
                    low = (value - high.astype(F32)).astype(BF16)
                    w[j, 16 * a : 16 * a + 16, 0:128] = high
                    w[j, 16 * a : 16 * a + 16, 128:256] = low
                sides = []
                for side in range(2):
                    x0 = xf[side, pl.ds(row0, 64, stride=CH), :].astype(BF16)
                    x1 = xf[side, pl.ds(row0 + 4, 64, stride=CH), :].astype(BF16)
                    sides.append(jnp.concatenate([x0, x1], 0))
                both = jnp.dot(jnp.concatenate(sides, 1), w[j], preferred_element_type=F32)
                both = both[:, :128] + both[:, 128:]
                out = jnp.where(lax.broadcasted_iota(jnp.int32, (64, 128), 1) < 64, both[:64], both[64:])
                for h in range(2):
                    for xx in range(NX):
                        sbuf[c, xx, pl.ds(g * 8 + h * 4 + j, NZ, stride=CH), :] = out[h * 32 + xx * NZ : h * 32 + xx * NZ + NZ]
            return 0

        lax.fori_loop(0, CH // 8, half, 0)

    def first_z_copy(d):
        to = lax.rem(z + d, NZ)
        return pltpu.make_async_remote_copy(
            src_ref=sbuf.at[0, :, pl.ds(pl.multiple_of(to * CH, CH), CH)], dst_ref=rz0.at[d - 1],
            send_sem=zs_sem.at[0, d - 1], recv_sem=zr_sem.at[0, d - 1],
            device_id={"ew": to * NX + x}, device_id_type=MESH)

    def first_x_copy(d):
        to = lax.rem(x + d, NX)
        return pltpu.make_async_remote_copy(
            src_ref=sum0.at[to], dst_ref=rx0.at[d - 1],
            send_sem=x0s_sem.at[d - 1], recv_sem=x0r_sem.at[d - 1],
            device_id={"ew": z * NX + to}, device_id_type=MESH)

    grid_copy0.wait()
    compute(0, gridv0, 0)
    pl.semaphore_wait(barrier, NX - 1 + NZ - 1 + NS - 1)
    for d in range(1, NZ):
        first_z_copy(d).start()
    grid_copy.wait()

    def chunk(c, _):
        compute(c, gridv, pl.multiple_of(c * CH - CH, CH))
        for side in (0, 1):
            far_copy(c, side).start()
            near_copy(c, side, 1 - side).start()

        @pl.when(c >= 3)
        def _():
            pass_on(c - 2)

        return 0

    lax.fori_loop(1, chunks, chunk, 0)

    pass_on(chunks - 2)
    along_z(1)
    pass_on(chunks - 1)
    along_z(2)
    for d in range(1, NZ):
        first_z_copy(d).wait_recv()
    total = sbuf[0, :, pl.ds(pl.multiple_of(z * CH, CH), CH), :]
    for d in range(NZ - 1):
        total = total + rz0[d]
    sum0[...] = total
    for d in range(1, NX):
        first_x_copy(d).start()

    def second(c, _):
        along_z(c)
        return 0

    lax.fori_loop(3, chunks, second, 0)

    for copy in leg_copies:
        copy.wait()

    def split(i, _):
        at = pl.ds(pl.multiple_of(i * 128, 128), 128)
        value = legv[i].T
        high = value.astype(BF16)
        leghi[at, :] = high
        leglo[at, :] = (value - high.astype(F32)).astype(BF16)
        return 0

    lax.fori_loop(0, legv.shape[0], split, 0)

    sub8 = lax.broadcasted_iota(jnp.int32, (8, 128), 0)
    lane8 = lax.broadcasted_iota(jnp.int32, (8, 128), 1)
    obuf[...] = jnp.zeros_like(obuf)

    def place(c, total):
        for g in range(CH // 8):
            o = total[g * 8 : g * 8 + 8]
            r = pltpu.roll(o, 4, 0)
            o = jnp.where(sub8 < 4, o + r, r - o)
            r = pltpu.roll(pltpu.roll(o, 4, 0), 64, 1)
            o = jnp.where((sub8 < 4) == (lane8 < 64), o, r)
            obuf[pl.ds(pl.multiple_of(c * CH + g * 8, 8), 8), :] = o

    for d in range(1, NX):
        first_x_copy(d).wait_recv()
    place(0, sum0[x] + rx0[0] + rx0[1] + rx0[2])

    def third(c, _):
        for d in range(1, NZ):
            z_copy(c, d).wait_recv()
        total = zbuf[c, pl.ds(pl.multiple_of(z * CH, CH), CH)]
        for d in range(NZ - 1):
            total = total + rz[c, d]
        place(c, total)
        return 0

    lax.fori_loop(1, chunks, third, 0)

    turned = obuf[...].T
    for p in range(NS):
        ybuf[p] = jnp.concatenate([turned[4 * p : 4 * p + 4], turned[64 + 4 * p : 68 + 4 * p]], 0)
    for d in range(1, NS):
        y_copy(d).start()
    ry[ns] = ybuf[ns]

    columns = leghi.shape[1]
    column = lax.broadcasted_iota(jnp.int32, (2, columns), 1)
    wavenum = waves_s[ns]
    in_first = column <= truncation - wavenum
    shifted = jnp.where(in_first, column, column - (truncation - wavenum + 1))
    even = (shifted & 1) == 0
    degree = jnp.where(in_first, wavenum + column, column - 1).astype(F32)
    field_type = lax.div(order_s[ew], levels)
    power, bits = power_s[0], bits_s[0]
    for t in range(1, bits_s.shape[0]):
        power = jnp.where(field_type == t, power_s[t], power)
        bits = jnp.where(field_type == t, bits_s[t], bits)
    weight = jnp.exp(power * jnp.log(degree * (degree + 1.0) + 2.0))
    spread = (lax.shift_left(jnp.int32(1), bits) - 1).astype(F32) * (1.0 / 4096.0)

    def sent(c, _):
        for side in (0, 1):
            far_copy(c, side).wait_send()
            for part in (0, 1):
                near_copy(c, side, part).wait_send()
        for d in range(1, NZ):
            z_copy(c, d).wait_send()
        return 0

    lax.fori_loop(1, chunks, sent, 0)
    for d in range(1, NZ):
        first_z_copy(d).wait_send()
    for d in range(1, NX):
        first_x_copy(d).wait_send()
    for d in range(1, NS):
        y_copy(d).wait_recv()
    pieces = [None] * (rows * NS // 128)
    for i in range(NS):
        at, off = divmod(i * rows, 128)
        value = ry[i] if off == 0 else pltpu.roll(ry[i], off, 1)
        if off + rows <= 128:
            parts = [(at, value)]
        else:
            parts = [(at, jnp.where(lane8 >= off, value, 0.0)), (at + 1, jnp.where(lane8 < off, value, 0.0))]
        for k, v in parts:
            pieces[k] = v if pieces[k] is None else pieces[k] + v
    stacked = jnp.concatenate(pieces, 1)
    high = stacked.astype(BF16).astype(F32)
    both = jnp.concatenate([high, stacked - high], 0).astype(BF16)
    by_high = jnp.dot(both, leghi[...], preferred_element_type=F32)
    by_low = jnp.dot(both, leglo[...], preferred_element_type=F32)
    result = by_high[:8] + by_high[8:] + by_low[:8]

    chosen = jnp.where(
        in_first,
        jnp.where(even, result[0:2], result[4:6]),
        jnp.where(even, result[2:4], result[6:8]),
    )
    scaled = chosen * weight
    most = jnp.max(jnp.max(scaled, axis=0, keepdims=True), axis=1, keepdims=True)
    least = jnp.min(jnp.min(scaled, axis=0, keepdims=True), axis=1, keepdims=True)
    rmm[0, 0:1] = jnp.where(lane8[0:1] < 64, most, -least)
    for d in range(1, NS):
        m_copy(d).start()
    for d in range(1, NS):
        y_copy(d).wait_send()
    for d in range(1, NS):
        m_copy(d).wait_recv()
    top = rmm[0, 0:1]
    for d in range(1, NS):
        top = jnp.maximum(top, rmm[d, 0:1])
    highest = top[:, 0:1]
    lowest = -top[:, 64:65]
    span = highest - lowest + 1e-6
    out_ref[0, 0] = (scaled - lowest) / span * spread

    for d in range(1, NS):
        m_copy(d).wait_send()


def shards(grid, band_rows, wave_pairs, packer_order, field_bits, field_power, legendre):
    fields, hemis, rows, points = grid.shape
    lats, columns = legendre.shape[1:]
    truncation = columns - 2
    levels = fields // field_bits.shape[0]
    chunks = rows // CH
    smem = pl.BlockSpec(memory_space=pltpu.SMEM)
    hbm = pl.BlockSpec(memory_space=pltpu.HBM)
    dma = pltpu.SemaphoreType.DMA
    return pl.pallas_call(
        functools.partial(kernel, truncation, levels),
        out_shape=jax.ShapeDtypeStruct((1, 1, 2, columns), F32),
        in_specs=[smem] * 5 + [hbm] * 2,
        out_specs=pl.BlockSpec(memory_space=pltpu.VMEM),
        scratch_shapes=[
            pltpu.VMEM((fields, hemis, CH, points), BF16),
            pltpu.VMEM((fields, hemis, rows - CH, points), BF16),
            pltpu.VMEM((lats // 128, columns, 128), F32),
            pltpu.VMEM((lats, columns), BF16),
            pltpu.VMEM((lats, columns), BF16),
            pltpu.VMEM((2, fields * hemis * CH, 128), F32),
            pltpu.VMEM((4, 256, 256), BF16),
            pltpu.VMEM((4, 2, 16, 128), F32),
            pltpu.VMEM((chunks, NX, NZ * CH, 128), F32),
            pltpu.VMEM((chunks, 2, HALF, 128), F32),
            pltpu.VMEM((chunks, 2, NZ * CH, 128), F32),
            pltpu.VMEM((chunks, NZ * CH, 128), F32),
            pltpu.VMEM((chunks, NZ - 1, CH, 128), F32),
            pltpu.VMEM((NZ - 1, NX, CH, 128), F32),
            pltpu.VMEM((NX, CH, 128), F32),
            pltpu.VMEM((NX - 1, CH, 128), F32),
            pltpu.VMEM((128, 128), F32),
            pltpu.VMEM((NS, 8, 128), F32),
            pltpu.VMEM((NS, 8, 128), F32),
            pltpu.VMEM((NS, 8, 128), F32),
            dma((2,)),
            dma((lats // 128,)),
            dma((chunks, 2)),
            dma((chunks, 2)),
            dma((chunks, 2, 2)),
            dma((chunks, 2, 2)),
            dma((NX - 1,)),
            dma((NX - 1,)),
            dma((chunks, NZ - 1)),
            dma((chunks, NZ - 1)),
            dma((NS - 1,)),
            dma((NS - 1,)),
            dma((NS - 1,)),
            dma((NS - 1,)),
        ],
        compiler_params=pltpu.CompilerParams(
            collective_id=0, has_side_effects=True, vmem_limit_bytes=61 * 2**20
        ),
    )(band_rows, wave_pairs, packer_order, field_bits, field_power, grid, jnp.transpose(legendre, (2, 0, 1)))


def solution(mesh):
    return jax.shard_map(
        shards,
        mesh=mesh,
        in_specs=(P(None, None, "ns", "ew"), P(), P(), P(), P(), P(), P("ns", None, None)),
        out_specs=P("ew", "ns", None, None),
        check_vma=False,
    )
```

```python
import functools

import jax
import jax.numpy as jnp
import numpy as np
from jax import lax
from jax.experimental import pallas as pl
from jax.experimental.pallas import tpu as pltpu
from jax.sharding import PartitionSpec as P

MESH = pl.DeviceIdType.MESH
NX = 4
NZ = 8
NS = 16
CH = 16
HALF = NZ * CH // 2
F32 = jnp.float32
BF16 = jnp.bfloat16


def _fit(function, terms):
    z = 0.125 + 0.125 * np.cos(np.pi * (np.arange(200) + 0.5) / 200)
    cheb = np.polynomial.chebyshev.Chebyshev.fit(z, function(np.sqrt(z)), terms - 1, domain=[0, 0.25])
    return [float(v) for v in cheb.convert(kind=np.polynomial.Polynomial).coef]


COS = _fit(lambda t: np.cos(2 * np.pi * t), 7)
SIN = _fit(lambda t: np.sin(2 * np.pi * t) / t, 7)


def _horner(coefs, z):
    total = jnp.full_like(z, coefs[-1])
    for c in coefs[-2::-1]:
        total = total * z + c
    return total


def _cos_sin(product, length, inverse):
    rest = product - jnp.round(product * inverse) * length
    t = rest * inverse
    z = t * t
    return _horner(COS, z), t * _horner(SIN, z)


def kernel(
    truncation, levels,
    band_hbm, waves_hbm, order_hbm, bits_hbm, power_hbm, grid_hbm, leg_hbm,
    out_ref,
    band_s, waves_s, order_s, bits_s, power_s,
    gridv0, gridv, legv, leghi, leglo, xf, w, cs, sbuf, rfar, rx, zbuf, rz, rz0, sum0, rx0, obuf, ybuf, ry, rmm,
    small_sem, grid_sem, leg_sem, fs_sem, fr_sem, xs_sem, xr_sem, x0s_sem, x0r_sem, zs_sem, zr_sem, ys_sem, yr_sem, ms_sem, mr_sem,
):
    ew, ns = lax.axis_index("ew"), lax.axis_index("ns")
    x, z = lax.rem(ew, NX), lax.div(ew, NX)
    rows, points = grid_hbm.shape[2:]
    chunks = rows // CH

    small_copies = [
        pltpu.make_async_copy(a, b, small_sem.at[i])
        for i, (a, b) in enumerate(
            ((waves_hbm, waves_s), (band_hbm, band_s), (order_hbm, order_s), (bits_hbm, bits_s), (power_hbm, power_s)))
    ]
    for copy in small_copies:
        copy.start()
    grid_copy0 = pltpu.make_async_copy(grid_hbm.at[:, :, 0:CH], gridv0, grid_sem.at[0])
    grid_copy0.start()
    grid_copy = pltpu.make_async_copy(grid_hbm.at[:, :, CH:rows], gridv, grid_sem.at[1])
    grid_copy.start()
    leg_copies = [
        pltpu.make_async_copy(leg_hbm.at[:, 0, k * 128 : (k + 1) * 128], legv.at[k], leg_sem.at[k])
        for k in range(legv.shape[0])
    ]
    for copy in leg_copies:
        copy.start()

    barrier = pltpu.get_barrier_semaphore()
    for d in range(1, NX):
        pl.semaphore_signal(barrier, inc=1, device_id={"ew": z * NX + lax.rem(x + d, NX)}, device_id_type=MESH)
    for d in range(1, NZ):
        pl.semaphore_signal(barrier, inc=1, device_id={"ew": lax.rem(z + d, NZ) * NX + x}, device_id_type=MESH)
    for d in range(1, NS):
        pl.semaphore_signal(barrier, inc=1, device_id={"ns": lax.rem(ns + d, NS)}, device_id_type=MESH)

    w[...] = jnp.zeros_like(w)
    xf[1] = jnp.zeros_like(xf[1])

    for copy in small_copies:
        copy.wait()

    lane = lax.broadcasted_iota(jnp.int32, (16, 128), 1)
    sub16 = lax.broadcasted_iota(jnp.int32, (16, 128), 0)
    pair_of = (lane & 63) >> 2
    wave = jnp.zeros((16, 128), jnp.int32)
    for p in range(16):
        wave = jnp.where(pair_of == p, waves_s[p], wave)
    wave = jnp.where((lane & 2) == 0, wave, truncation - wave).astype(F32)
    imaginary = (lane & 1) == 1
    low_half = lane < 64
    first = ew * points
    product_a = wave * (first + 16 * sub16).astype(F32)
    product_b = wave * sub16.astype(F32)
    point0 = (first + sub16).astype(F32)
    point_end = (first + points).astype(F32)

    def neighbour(side):
        return lax.rem(x + (1 if side == 0 else NX - 1), NX)

    def far_copy(c, side):
        return pltpu.make_async_remote_copy(
            src_ref=sbuf.at[c, lax.rem(x + 2, NX), pl.ds(side * HALF, HALF)], dst_ref=rfar.at[c, side],
            send_sem=fs_sem.at[c, side], recv_sem=fr_sem.at[c, side],
            device_id={"ew": z * NX + neighbour(side)}, device_id_type=MESH)

    def near_copy(c, side, part):
        rows = pl.ds(part * HALF, HALF)
        return pltpu.make_async_remote_copy(
            src_ref=sbuf.at[c, neighbour(side), rows], dst_ref=rx.at[c, side, rows],
            send_sem=xs_sem.at[c, side, part], recv_sem=xr_sem.at[c, side, part],
            device_id={"ew": z * NX + neighbour(side)}, device_id_type=MESH)

    def z_copy(c, d):
        to = lax.rem(z + d, NZ)
        return pltpu.make_async_remote_copy(
            src_ref=zbuf.at[c, pl.ds(pl.multiple_of(to * CH, CH), CH)], dst_ref=rz.at[c, d - 1],
            send_sem=zs_sem.at[c, d - 1], recv_sem=zr_sem.at[c, d - 1],
            device_id={"ew": to * NX + x}, device_id_type=MESH)

    def y_copy(d):
        to = lax.rem(ns + d, NS)
        return pltpu.make_async_remote_copy(
            src_ref=ybuf.at[to], dst_ref=ry.at[ns],
            send_sem=ys_sem.at[d - 1], recv_sem=yr_sem.at[d - 1],
            device_id={"ns": to}, device_id_type=MESH)

    def m_copy(d):
        to = lax.rem(ns + d, NS)
        return pltpu.make_async_remote_copy(
            src_ref=rmm.at[0, 0:1], dst_ref=rmm.at[d, 0:1],
            send_sem=ms_sem.at[d - 1], recv_sem=mr_sem.at[d - 1],
            device_id={"ns": to}, device_id_type=MESH)

    def pass_on(c):
        for side in (0, 1):
            far_copy(c, side).wait_recv()
            rows = pl.ds(side * HALF, HALF)
            sbuf[c, neighbour(side), rows] = sbuf[c, neighbour(side), rows] + rfar[c, side]
            near_copy(c, side, side).start()

    def along_z(c):
        for side in (0, 1):
            for part in (0, 1):
                near_copy(c, side, part).wait_recv()
        zbuf[c] = sbuf[c, x] + rx[c, 0] + rx[c, 1]
        for d in range(1, NZ):
            z_copy(c, d).start()

    def compute(c, grid_ref, grid_row):
        def convert(zz, _):
            for xx in range(NX):
                field = order_s[zz * NX + xx]
                for h in range(2):
                    at = pl.multiple_of((h * 32 + xx * NZ + zz) * CH, CH)
                    block = grid_ref[field, h, pl.ds(grid_row, CH), :].astype(F32)
                    xf[0, pl.ds(at, CH), :] = block[:, 0:128]
                    xf[1, pl.ds(at, CH), 0 : points - 128] = block[:, 128:points]
            return 0

        lax.fori_loop(0, NZ, convert, 0)

        def half(g, _):
            for j in range(4):
                row0 = g * 8 + j
                band0 = band_s[ns * rows + c * CH + row0]
                band1 = band_s[ns * rows + c * CH + row0 + 4]
                length = jnp.where(low_half, 20 + 4 * band0, 20 + 4 * band1).astype(F32)
                inverse = 1.0 / length
                cos_a, sin_a = _cos_sin(product_a, length, inverse)
                cos_b, sin_b = _cos_sin(product_b, length, inverse)
                cs[j, 0] = jnp.where(imaginary, -sin_a, cos_a) * inverse
                cs[j, 1] = jnp.where(imaginary, cos_a, sin_a) * inverse
                end = jnp.minimum(length, point_end) - point0
                for a in range(11):
                    value = cs[j, 0, a : a + 1, :] * cos_b - cs[j, 1, a : a + 1, :] * sin_b
                    value = jnp.where(end > 16.0 * a, value, 0.0)
                    high = value.astype(BF16)
                    low = (value - high.astype(F32)).astype(BF16)
                    w[j, 16 * a : 16 * a + 16, 0:128] = high
                    w[j, 16 * a : 16 * a + 16, 128:256] = low
                sides = []
                for side in range(2):
                    x0 = xf[side, pl.ds(row0, 64, stride=CH), :].astype(BF16)
                    x1 = xf[side, pl.ds(row0 + 4, 64, stride=CH), :].astype(BF16)
                    sides.append(jnp.concatenate([x0, x1], 0))
                both = jnp.dot(jnp.concatenate(sides, 1), w[j], preferred_element_type=F32)
                both = both[:, :128] + both[:, 128:]
                out = jnp.where(lax.broadcasted_iota(jnp.int32, (64, 128), 1) < 64, both[:64], both[64:])
                for h in range(2):
                    for xx in range(NX):
                        sbuf[c, xx, pl.ds(g * 8 + h * 4 + j, NZ, stride=CH), :] = out[h * 32 + xx * NZ : h * 32 + xx * NZ + NZ]
            return 0

        lax.fori_loop(0, CH // 8, half, 0)

    def first_z_copy(d):
        to = lax.rem(z + d, NZ)
        return pltpu.make_async_remote_copy(
            src_ref=sbuf.at[1, :, pl.ds(pl.multiple_of(to * CH, CH), CH)], dst_ref=rz0.at[d - 1],
            send_sem=zs_sem.at[1, d - 1], recv_sem=zr_sem.at[1, d - 1],
            device_id={"ew": to * NX + x}, device_id_type=MESH)

    def first_x_copy(d):
        to = lax.rem(x + d, NX)
        return pltpu.make_async_remote_copy(
            src_ref=sum0.at[to], dst_ref=rx0.at[d - 1],
            send_sem=x0s_sem.at[d - 1], recv_sem=x0r_sem.at[d - 1],
            device_id={"ew": z * NX + to}, device_id_type=MESH)

    grid_copy0.wait()
    compute(0, gridv0, 0)
    pl.semaphore_wait(barrier, NX - 1 + NZ - 1 + NS - 1)
    def send_x(c):
        for side in (0, 1):
            far_copy(c, side).start()
            near_copy(c, side, 1 - side).start()

    send_x(0)
    grid_copy.wait()
    compute(1, gridv, 0)
    for d in range(1, NZ):
        first_z_copy(d).start()

    def chunk(c, _):
        compute(c, gridv, pl.multiple_of(c * CH - CH, CH))
        send_x(c)

        @pl.when(c != 3)
        def _():
            pass_on(c - 2)

        return 0

    lax.fori_loop(2, chunks, chunk, 0)

    pass_on(chunks - 2)
    along_z(0)
    pass_on(chunks - 1)
    along_z(2)
    for d in range(1, NZ):
        first_z_copy(d).wait_recv()
    total = sbuf[1, :, pl.ds(pl.multiple_of(z * CH, CH), CH), :]
    for d in range(NZ - 1):
        total = total + rz0[d]
    sum0[...] = total
    for d in range(1, NX):
        first_x_copy(d).start()

    def second(c, _):
        along_z(c)
        return 0

    lax.fori_loop(3, chunks, second, 0)

    for copy in leg_copies:
        copy.wait()

    def split(i, _):
        at = pl.ds(pl.multiple_of(i * 128, 128), 128)
        value = legv[i].T
        high = value.astype(BF16)
        leghi[at, :] = high
        leglo[at, :] = (value - high.astype(F32)).astype(BF16)
        return 0

    lax.fori_loop(0, legv.shape[0], split, 0)

    sub8 = lax.broadcasted_iota(jnp.int32, (8, 128), 0)
    lane8 = lax.broadcasted_iota(jnp.int32, (8, 128), 1)
    obuf[...] = jnp.zeros_like(obuf)

    def place(c, total):
        for g in range(CH // 8):
            o = total[g * 8 : g * 8 + 8]
            r = pltpu.roll(o, 4, 0)
            o = jnp.where(sub8 < 4, o + r, r - o)
            r = pltpu.roll(pltpu.roll(o, 4, 0), 64, 1)
            o = jnp.where((sub8 < 4) == (lane8 < 64), o, r)
            obuf[pl.ds(pl.multiple_of(c * CH + g * 8, 8), 8), :] = o

    for d in range(1, NX):
        first_x_copy(d).wait_recv()
    place(1, sum0[x] + rx0[0] + rx0[1] + rx0[2])

    def third(i, _):
        c = i + lax.div(i + 2, 3)
        for d in range(1, NZ):
            z_copy(c, d).wait_recv()
        total = zbuf[c, pl.ds(pl.multiple_of(z * CH, CH), CH)]
        for d in range(NZ - 1):
            total = total + rz[c, d]
        place(c, total)
        return 0

    lax.fori_loop(0, chunks - 1, third, 0)

    turned = obuf[...].T
    for p in range(NS):
        ybuf[p] = jnp.concatenate([turned[4 * p : 4 * p + 4], turned[64 + 4 * p : 68 + 4 * p]], 0)
    for d in range(1, NS):
        y_copy(d).start()
    ry[ns] = ybuf[ns]

    columns = leghi.shape[1]
    column = lax.broadcasted_iota(jnp.int32, (2, columns), 1)
    wavenum = waves_s[ns]
    in_first = column <= truncation - wavenum
    shifted = jnp.where(in_first, column, column - (truncation - wavenum + 1))
    even = (shifted & 1) == 0
    degree = jnp.where(in_first, wavenum + column, column - 1).astype(F32)
    field_type = lax.div(order_s[ew], levels)
    power, bits = power_s[0], bits_s[0]
    for t in range(1, bits_s.shape[0]):
        power = jnp.where(field_type == t, power_s[t], power)
        bits = jnp.where(field_type == t, bits_s[t], bits)
    weight = jnp.exp(power * jnp.log(degree * (degree + 1.0) + 2.0))
    spread = (lax.shift_left(jnp.int32(1), bits) - 1).astype(F32) * (1.0 / 4096.0)

    def sent(i, _):
        c = i + lax.div(i + 2, 3)
        for side in (0, 1):
            far_copy(c, side).wait_send()
            for part in (0, 1):
                near_copy(c, side, part).wait_send()
        for d in range(1, NZ):
            z_copy(c, d).wait_send()
        return 0

    lax.fori_loop(0, chunks - 1, sent, 0)
    for d in range(1, NZ):
        first_z_copy(d).wait_send()
    for d in range(1, NX):
        first_x_copy(d).wait_send()
    for d in range(1, NS):
        y_copy(d).wait_recv()
    pieces = [None] * (rows * NS // 128)
    for i in range(NS):
        at, off = divmod(i * rows, 128)
        value = ry[i] if off == 0 else pltpu.roll(ry[i], off, 1)
        if off + rows <= 128:
            parts = [(at, value)]
        else:
            parts = [(at, jnp.where(lane8 >= off, value, 0.0)), (at + 1, jnp.where(lane8 < off, value, 0.0))]
        for k, v in parts:
            pieces[k] = v if pieces[k] is None else pieces[k] + v
    stacked = jnp.concatenate(pieces, 1)
    high = stacked.astype(BF16).astype(F32)
    both = jnp.concatenate([high, stacked - high], 0).astype(BF16)
    by_high = jnp.dot(both, leghi[...], preferred_element_type=F32)
    by_low = jnp.dot(both, leglo[...], preferred_element_type=F32)
    result = by_high[:8] + by_high[8:] + by_low[:8]

    chosen = jnp.where(
        in_first,
        jnp.where(even, result[0:2], result[4:6]),
        jnp.where(even, result[2:4], result[6:8]),
    )
    scaled = chosen * weight
    most = jnp.max(jnp.max(scaled, axis=0, keepdims=True), axis=1, keepdims=True)
    least = jnp.min(jnp.min(scaled, axis=0, keepdims=True), axis=1, keepdims=True)
    rmm[0, 0:1] = jnp.where(lane8[0:1] < 64, most, -least)
    for d in range(1, NS):
        m_copy(d).start()
    for d in range(1, NS):
        y_copy(d).wait_send()
    for d in range(1, NS):
        m_copy(d).wait_recv()
    top = rmm[0, 0:1]
    for d in range(1, NS):
        top = jnp.maximum(top, rmm[d, 0:1])
    highest = top[:, 0:1]
    lowest = -top[:, 64:65]
    span = highest - lowest + 1e-6
    out_ref[0, 0] = (scaled - lowest) / span * spread

    for d in range(1, NS):
        m_copy(d).wait_send()


def shards(grid, band_rows, wave_pairs, packer_order, field_bits, field_power, legendre):
    fields, hemis, rows, points = grid.shape
    lats, columns = legendre.shape[1:]
    truncation = columns - 2
    levels = fields // field_bits.shape[0]
    chunks = rows // CH
    hbm = pl.BlockSpec(memory_space=pltpu.HBM)
    dma = pltpu.SemaphoreType.DMA
    return pl.pallas_call(
        functools.partial(kernel, truncation, levels),
        out_shape=jax.ShapeDtypeStruct((1, 1, 2, columns), F32),
        in_specs=[hbm] * 7,
        out_specs=pl.BlockSpec(memory_space=pltpu.VMEM),
        scratch_shapes=[
            pltpu.SMEM(band_rows.shape, jnp.int32),
            pltpu.SMEM(wave_pairs.shape, jnp.int32),
            pltpu.SMEM(packer_order.shape, jnp.int32),
            pltpu.SMEM(field_bits.shape, jnp.int32),
            pltpu.SMEM(field_power.shape, F32),
            pltpu.VMEM((fields, hemis, CH, points), BF16),
            pltpu.VMEM((fields, hemis, rows - CH, points), BF16),
            pltpu.VMEM((lats // 128, columns, 128), F32),
            pltpu.VMEM((lats, columns), BF16),
            pltpu.VMEM((lats, columns), BF16),
            pltpu.VMEM((2, fields * hemis * CH, 128), F32),
            pltpu.VMEM((4, 256, 256), BF16),
            pltpu.VMEM((4, 2, 16, 128), F32),
            pltpu.VMEM((chunks, NX, NZ * CH, 128), F32),
            pltpu.VMEM((chunks, 2, HALF, 128), F32),
            pltpu.VMEM((chunks, 2, NZ * CH, 128), F32),
            pltpu.VMEM((chunks, NZ * CH, 128), F32),
            pltpu.VMEM((chunks, NZ - 1, CH, 128), F32),
            pltpu.VMEM((NZ - 1, NX, CH, 128), F32),
            pltpu.VMEM((NX, CH, 128), F32),
            pltpu.VMEM((NX - 1, CH, 128), F32),
            pltpu.VMEM((128, 128), F32),
            pltpu.VMEM((NS, 8, 128), F32),
            pltpu.VMEM((NS, 8, 128), F32),
            pltpu.VMEM((NS, 8, 128), F32),
            dma((5,)),
            dma((2,)),
            dma((lats // 128,)),
            dma((chunks, 2)),
            dma((chunks, 2)),
            dma((chunks, 2, 2)),
            dma((chunks, 2, 2)),
            dma((NX - 1,)),
            dma((NX - 1,)),
            dma((chunks, NZ - 1)),
            dma((chunks, NZ - 1)),
            dma((NS - 1,)),
            dma((NS - 1,)),
            dma((NS - 1,)),
            dma((NS - 1,)),
        ],
        compiler_params=pltpu.CompilerParams(
            collective_id=0, has_side_effects=True, vmem_limit_bytes=61 * 2**20
        ),
    )(band_rows, wave_pairs, packer_order, field_bits, field_power, grid, jnp.transpose(legendre, (2, 0, 1)))


def solution(mesh):
    return jax.shard_map(
        shards,
        mesh=mesh,
        in_specs=(P(None, None, "ns", "ew"), P(), P(), P(), P(), P(), P("ns", None, None)),
        out_specs=P("ew", "ns", None, None),
        check_vma=False,
    )
```

```python
import functools

import jax
import jax.numpy as jnp
import numpy as np
from jax import lax
from jax.experimental import pallas as pl
from jax.experimental.pallas import tpu as pltpu
from jax.sharding import PartitionSpec as P

MESH = pl.DeviceIdType.MESH
NX = 4
NZ = 8
NS = 16
CH = 16
HALF = NZ * CH // 2
FAR_Z = (4, 3, 5, 2, 6, 1, 7)
FAR_NS = (8, 7, 9, 6, 10, 5, 11, 4, 12, 3, 13, 2, 14, 1, 15)
F32 = jnp.float32
BF16 = jnp.bfloat16


def _fit(function, terms):
    z = 0.125 + 0.125 * np.cos(np.pi * (np.arange(200) + 0.5) / 200)
    cheb = np.polynomial.chebyshev.Chebyshev.fit(z, function(np.sqrt(z)), terms - 1, domain=[0, 0.25])
    return [float(v) for v in cheb.convert(kind=np.polynomial.Polynomial).coef]


COS = _fit(lambda t: np.cos(2 * np.pi * t), 7)
SIN = _fit(lambda t: np.sin(2 * np.pi * t) / t, 7)


def _horner(coefs, z):
    total = jnp.full_like(z, coefs[-1])
    for c in coefs[-2::-1]:
        total = total * z + c
    return total


def _cos_sin(product, length, inverse):
    rest = product - jnp.round(product * inverse) * length
    t = rest * inverse
    z = t * t
    return _horner(COS, z), t * _horner(SIN, z)


def kernel(
    truncation, levels,
    band_hbm, waves_hbm, order_hbm, bits_hbm, power_hbm, grid_hbm, leg_hbm,
    out_ref,
    band_s, waves_s, order_s, bits_s, power_s,
    gridv0, gridv, legv, leghi, leglo, xf, w, cs, sbuf, rfar, rx, zbuf, rz, rz0, sum0, rx0, obuf, ybuf, ry, rmm,
    small_sem, grid_sem, leg_sem, fs_sem, fr_sem, xs_sem, xr_sem, x0s_sem, x0r_sem, zs_sem, zr_sem, ys_sem, yr_sem, ms_sem, mr_sem,
):
    ew, ns = lax.axis_index("ew"), lax.axis_index("ns")
    x, z = lax.rem(ew, NX), lax.div(ew, NX)
    rows, points = grid_hbm.shape[2:]
    chunks = rows // CH

    small_copies = [
        pltpu.make_async_copy(a, b, small_sem.at[i])
        for i, (a, b) in enumerate(
            ((waves_hbm, waves_s), (band_hbm, band_s), (order_hbm, order_s), (bits_hbm, bits_s), (power_hbm, power_s)))
    ]
    for copy in small_copies:
        copy.start()
    grid_copy0 = pltpu.make_async_copy(grid_hbm.at[:, :, 0:CH], gridv0, grid_sem.at[0])
    grid_copy0.start()
    grid_copy = pltpu.make_async_copy(grid_hbm.at[:, :, CH:rows], gridv, grid_sem.at[1])
    grid_copy.start()
    leg_copies = [
        pltpu.make_async_copy(leg_hbm.at[:, 0, k * 128 : (k + 1) * 128], legv.at[k], leg_sem.at[k])
        for k in range(legv.shape[0])
    ]
    for copy in leg_copies:
        copy.start()

    barrier = pltpu.get_barrier_semaphore()
    for d in FAR_NS:
        pl.semaphore_signal(barrier, inc=1, device_id={"ns": lax.rem(ns + d, NS)}, device_id_type=MESH)
    for d in FAR_Z:
        pl.semaphore_signal(barrier, inc=1, device_id={"ew": lax.rem(z + d, NZ) * NX + x}, device_id_type=MESH)
    for d in range(1, NX):
        pl.semaphore_signal(barrier, inc=1, device_id={"ew": z * NX + lax.rem(x + d, NX)}, device_id_type=MESH)

    w[...] = jnp.zeros_like(w)
    xf[1] = jnp.zeros_like(xf[1])

    for copy in small_copies:
        copy.wait()

    lane = lax.broadcasted_iota(jnp.int32, (16, 128), 1)
    sub16 = lax.broadcasted_iota(jnp.int32, (16, 128), 0)
    pair_of = (lane & 63) >> 2
    wave = jnp.zeros((16, 128), jnp.int32)
    for p in range(16):
        wave = jnp.where(pair_of == p, waves_s[p], wave)
    wave = jnp.where((lane & 2) == 0, wave, truncation - wave).astype(F32)
    imaginary = (lane & 1) == 1
    low_half = lane < 64
    first = ew * points
    product_a = wave * (first + 16 * sub16).astype(F32)
    product_b = wave * sub16.astype(F32)
    point0 = (first + sub16).astype(F32)
    point_end = (first + points).astype(F32)

    def neighbour(side):
        return lax.rem(x + (1 if side == 0 else NX - 1), NX)

    def far_copy(c, side):
        return pltpu.make_async_remote_copy(
            src_ref=sbuf.at[c, lax.rem(x + 2, NX), pl.ds(side * HALF, HALF)], dst_ref=rfar.at[c, side],
            send_sem=fs_sem.at[c, side], recv_sem=fr_sem.at[c, side],
            device_id={"ew": z * NX + neighbour(side)}, device_id_type=MESH)

    def near_copy(c, side, part):
        rows = pl.ds(part * HALF, HALF)
        return pltpu.make_async_remote_copy(
            src_ref=sbuf.at[c, neighbour(side), rows], dst_ref=rx.at[c, side, rows],
            send_sem=xs_sem.at[c, side, part], recv_sem=xr_sem.at[c, side, part],
            device_id={"ew": z * NX + neighbour(side)}, device_id_type=MESH)

    def z_copy(c, d):
        to = lax.rem(z + d, NZ)
        return pltpu.make_async_remote_copy(
            src_ref=zbuf.at[c, pl.ds(pl.multiple_of(to * CH, CH), CH)], dst_ref=rz.at[c, d - 1],
            send_sem=zs_sem.at[c, d - 1], recv_sem=zr_sem.at[c, d - 1],
            device_id={"ew": to * NX + x}, device_id_type=MESH)

    def y_copy(d):
        to = lax.rem(ns + d, NS)
        return pltpu.make_async_remote_copy(
            src_ref=ybuf.at[to], dst_ref=ry.at[ns],
            send_sem=ys_sem.at[d - 1], recv_sem=yr_sem.at[d - 1],
            device_id={"ns": to}, device_id_type=MESH)

    def m_copy(d):
        to = lax.rem(ns + d, NS)
        return pltpu.make_async_remote_copy(
            src_ref=rmm.at[0, 0:1], dst_ref=rmm.at[d, 0:1],
            send_sem=ms_sem.at[d - 1], recv_sem=mr_sem.at[d - 1],
            device_id={"ns": to}, device_id_type=MESH)

    def pass_on(c):
        for side in (0, 1):
            far_copy(c, side).wait_recv()
            rows = pl.ds(side * HALF, HALF)
            sbuf[c, neighbour(side), rows] = sbuf[c, neighbour(side), rows] + rfar[c, side]
            near_copy(c, side, side).start()

    def along_z(c):
        for side in (0, 1):
            for part in (0, 1):
                near_copy(c, side, part).wait_recv()
        zbuf[c] = sbuf[c, x] + rx[c, 0] + rx[c, 1]
        for d in FAR_Z:
            z_copy(c, d).start()

    def compute(c, grid_ref, grid_row):
        def convert(zz, _):
            for xx in range(NX):
                field = order_s[zz * NX + xx]
                for h in range(2):
                    at = pl.multiple_of((h * 32 + xx * NZ + zz) * CH, CH)
                    block = grid_ref[field, h, pl.ds(grid_row, CH), :].astype(F32)
                    xf[0, pl.ds(at, CH), :] = block[:, 0:128]
                    xf[1, pl.ds(at, CH), 0 : points - 128] = block[:, 128:points]
            return 0

        lax.fori_loop(0, NZ, convert, 0)

        def half(g, _):
            for j in range(4):
                row0 = g * 8 + j
                band0 = band_s[ns * rows + c * CH + row0]
                band1 = band_s[ns * rows + c * CH + row0 + 4]
                length = jnp.where(low_half, 20 + 4 * band0, 20 + 4 * band1).astype(F32)
                inverse = 1.0 / length
                cos_a, sin_a = _cos_sin(product_a, length, inverse)
                cos_b, sin_b = _cos_sin(product_b, length, inverse)
                cs[j, 0] = jnp.where(imaginary, -sin_a, cos_a) * inverse
                cs[j, 1] = jnp.where(imaginary, cos_a, sin_a) * inverse
                end = jnp.minimum(length, point_end) - point0
                for a in range(11):
                    value = cs[j, 0, a : a + 1, :] * cos_b - cs[j, 1, a : a + 1, :] * sin_b
                    value = jnp.where(end > 16.0 * a, value, 0.0)
                    high = value.astype(BF16)
                    low = (value - high.astype(F32)).astype(BF16)
                    w[j, 16 * a : 16 * a + 16, 0:128] = high
                    w[j, 16 * a : 16 * a + 16, 128:256] = low
                sides = []
                for side in range(2):
                    x0 = xf[side, pl.ds(row0, 64, stride=CH), :].astype(BF16)
                    x1 = xf[side, pl.ds(row0 + 4, 64, stride=CH), :].astype(BF16)
                    sides.append(jnp.concatenate([x0, x1], 0))
                both = jnp.dot(jnp.concatenate(sides, 1), w[j], preferred_element_type=F32)
                both = both[:, :128] + both[:, 128:]
                out = jnp.where(lax.broadcasted_iota(jnp.int32, (64, 128), 1) < 64, both[:64], both[64:])
                for h in range(2):
                    for xx in range(NX):
                        sbuf[c, xx, pl.ds(g * 8 + h * 4 + j, NZ, stride=CH), :] = out[h * 32 + xx * NZ : h * 32 + xx * NZ + NZ]
            return 0

        lax.fori_loop(0, CH // 8, half, 0)

    def first_z_copy(d):
        to = lax.rem(z + d, NZ)
        return pltpu.make_async_remote_copy(
            src_ref=sbuf.at[1, :, pl.ds(pl.multiple_of(to * CH, CH), CH)], dst_ref=rz0.at[d - 1],
            send_sem=zs_sem.at[1, d - 1], recv_sem=zr_sem.at[1, d - 1],
            device_id={"ew": to * NX + x}, device_id_type=MESH)

    def first_x_copy(d):
        to = lax.rem(x + d, NX)
        return pltpu.make_async_remote_copy(
            src_ref=sum0.at[to], dst_ref=rx0.at[d - 1],
            send_sem=x0s_sem.at[d - 1], recv_sem=x0r_sem.at[d - 1],
            device_id={"ew": z * NX + to}, device_id_type=MESH)

    grid_copy0.wait()
    compute(0, gridv0, 0)
    pl.semaphore_wait(barrier, NX - 1 + NZ - 1 + NS - 1)
    def send_x(c):
        for side in (0, 1):
            far_copy(c, side).start()
            near_copy(c, side, 1 - side).start()

    send_x(0)
    grid_copy.wait()
    compute(1, gridv, 0)
    for d in FAR_Z:
        first_z_copy(d).start()

    def chunk(c, _):
        compute(c, gridv, pl.multiple_of(c * CH - CH, CH))
        send_x(c)

        @pl.when(c != 3)
        def _():
            pass_on(c - 2)

        return 0

    lax.fori_loop(2, chunks, chunk, 0)

    pass_on(chunks - 2)
    along_z(0)
    pass_on(chunks - 1)
    along_z(2)
    for d in range(1, NZ):
        first_z_copy(d).wait_recv()
    total = sbuf[1, :, pl.ds(pl.multiple_of(z * CH, CH), CH), :]
    for d in range(NZ - 1):
        total = total + rz0[d]
    sum0[...] = total
    for d in range(1, NX):
        first_x_copy(d).start()

    def second(c, _):
        along_z(c)
        return 0

    lax.fori_loop(3, chunks, second, 0)

    for copy in leg_copies:
        copy.wait()

    def split(i, _):
        at = pl.ds(pl.multiple_of(i * 128, 128), 128)
        value = legv[i].T
        high = value.astype(BF16)
        leghi[at, :] = high
        leglo[at, :] = (value - high.astype(F32)).astype(BF16)
        return 0

    lax.fori_loop(0, legv.shape[0], split, 0)

    sub8 = lax.broadcasted_iota(jnp.int32, (8, 128), 0)
    lane8 = lax.broadcasted_iota(jnp.int32, (8, 128), 1)
    obuf[...] = jnp.zeros_like(obuf)

    def place(c, total):
        for g in range(CH // 8):
            o = total[g * 8 : g * 8 + 8]
            r = pltpu.roll(o, 4, 0)
            o = jnp.where(sub8 < 4, o + r, r - o)
            r = pltpu.roll(pltpu.roll(o, 4, 0), 64, 1)
            o = jnp.where((sub8 < 4) == (lane8 < 64), o, r)
            obuf[pl.ds(pl.multiple_of(c * CH + g * 8, 8), 8), :] = o

    for d in range(1, NX):
        first_x_copy(d).wait_recv()
    place(1, sum0[x] + rx0[0] + rx0[1] + rx0[2])

    def third(i, _):
        c = i + lax.div(i + 2, 3)
        for d in range(1, NZ):
            z_copy(c, d).wait_recv()
        total = zbuf[c, pl.ds(pl.multiple_of(z * CH, CH), CH)]
        for d in range(NZ - 1):
            total = total + rz[c, d]
        place(c, total)
        return 0

    lax.fori_loop(0, chunks - 1, third, 0)

    turned = obuf[...].T
    for p in range(NS):
        ybuf[p] = jnp.concatenate([turned[4 * p : 4 * p + 4], turned[64 + 4 * p : 68 + 4 * p]], 0)
    for d in FAR_NS:
        y_copy(d).start()
    ry[ns] = ybuf[ns]

    columns = leghi.shape[1]
    column = lax.broadcasted_iota(jnp.int32, (2, columns), 1)
    wavenum = waves_s[ns]
    in_first = column <= truncation - wavenum
    shifted = jnp.where(in_first, column, column - (truncation - wavenum + 1))
    even = (shifted & 1) == 0
    degree = jnp.where(in_first, wavenum + column, column - 1).astype(F32)
    field_type = lax.div(order_s[ew], levels)
    power, bits = power_s[0], bits_s[0]
    for t in range(1, bits_s.shape[0]):
        power = jnp.where(field_type == t, power_s[t], power)
        bits = jnp.where(field_type == t, bits_s[t], bits)
    weight = jnp.exp(power * jnp.log(degree * (degree + 1.0) + 2.0))
    spread = (lax.shift_left(jnp.int32(1), bits) - 1).astype(F32) * (1.0 / 4096.0)

    def sent(i, _):
        c = i + lax.div(i + 2, 3)
        for side in (0, 1):
            far_copy(c, side).wait_send()
            for part in (0, 1):
                near_copy(c, side, part).wait_send()
        for d in range(1, NZ):
            z_copy(c, d).wait_send()
        return 0

    lax.fori_loop(0, chunks - 1, sent, 0)
    for d in range(1, NZ):
        first_z_copy(d).wait_send()
    for d in range(1, NX):
        first_x_copy(d).wait_send()
    for d in range(1, NS):
        y_copy(d).wait_recv()
    pieces = [None] * (rows * NS // 128)
    for i in range(NS):
        at, off = divmod(i * rows, 128)
        value = ry[i] if off == 0 else pltpu.roll(ry[i], off, 1)
        if off + rows <= 128:
            parts = [(at, value)]
        else:
            parts = [(at, jnp.where(lane8 >= off, value, 0.0)), (at + 1, jnp.where(lane8 < off, value, 0.0))]
        for k, v in parts:
            pieces[k] = v if pieces[k] is None else pieces[k] + v
    stacked = jnp.concatenate(pieces, 1)
    high = stacked.astype(BF16).astype(F32)
    both = jnp.concatenate([high, stacked - high], 0).astype(BF16)
    by_high = jnp.dot(both, leghi[...], preferred_element_type=F32)
    by_low = jnp.dot(both, leglo[...], preferred_element_type=F32)
    result = by_high[:8] + by_high[8:] + by_low[:8]

    chosen = jnp.where(
        in_first,
        jnp.where(even, result[0:2], result[4:6]),
        jnp.where(even, result[2:4], result[6:8]),
    )
    scaled = chosen * weight
    most = jnp.max(jnp.max(scaled, axis=0, keepdims=True), axis=1, keepdims=True)
    least = jnp.min(jnp.min(scaled, axis=0, keepdims=True), axis=1, keepdims=True)
    rmm[0, 0:1] = jnp.where(lane8[0:1] < 64, most, -least)
    for d in FAR_NS:
        m_copy(d).start()
    for d in range(1, NS):
        y_copy(d).wait_send()
    for d in range(1, NS):
        m_copy(d).wait_recv()
    top = rmm[0, 0:1]
    for d in range(1, NS):
        top = jnp.maximum(top, rmm[d, 0:1])
    highest = top[:, 0:1]
    lowest = -top[:, 64:65]
    span = highest - lowest + 1e-6
    out_ref[0, 0] = (scaled - lowest) / span * spread

    for d in range(1, NS):
        m_copy(d).wait_send()


def shards(grid, band_rows, wave_pairs, packer_order, field_bits, field_power, legendre):
    fields, hemis, rows, points = grid.shape
    lats, columns = legendre.shape[1:]
    truncation = columns - 2
    levels = fields // field_bits.shape[0]
    chunks = rows // CH
    hbm = pl.BlockSpec(memory_space=pltpu.HBM)
    dma = pltpu.SemaphoreType.DMA
    return pl.pallas_call(
        functools.partial(kernel, truncation, levels),
        out_shape=jax.ShapeDtypeStruct((1, 1, 2, columns), F32),
        in_specs=[hbm] * 7,
        out_specs=pl.BlockSpec(memory_space=pltpu.VMEM),
        scratch_shapes=[
            pltpu.SMEM(band_rows.shape, jnp.int32),
            pltpu.SMEM(wave_pairs.shape, jnp.int32),
            pltpu.SMEM(packer_order.shape, jnp.int32),
            pltpu.SMEM(field_bits.shape, jnp.int32),
            pltpu.SMEM(field_power.shape, F32),
            pltpu.VMEM((fields, hemis, CH, points), BF16),
            pltpu.VMEM((fields, hemis, rows - CH, points), BF16),
            pltpu.VMEM((lats // 128, columns, 128), F32),
            pltpu.VMEM((lats, columns), BF16),
            pltpu.VMEM((lats, columns), BF16),
            pltpu.VMEM((2, fields * hemis * CH, 128), F32),
            pltpu.VMEM((4, 256, 256), BF16),
            pltpu.VMEM((4, 2, 16, 128), F32),
            pltpu.VMEM((chunks, NX, NZ * CH, 128), F32),
            pltpu.VMEM((chunks, 2, HALF, 128), F32),
            pltpu.VMEM((chunks, 2, NZ * CH, 128), F32),
            pltpu.VMEM((chunks, NZ * CH, 128), F32),
            pltpu.VMEM((chunks, NZ - 1, CH, 128), F32),
            pltpu.VMEM((NZ - 1, NX, CH, 128), F32),
            pltpu.VMEM((NX, CH, 128), F32),
            pltpu.VMEM((NX - 1, CH, 128), F32),
            pltpu.VMEM((128, 128), F32),
            pltpu.VMEM((NS, 8, 128), F32),
            pltpu.VMEM((NS, 8, 128), F32),
            pltpu.VMEM((NS, 8, 128), F32),
            dma((5,)),
            dma((2,)),
            dma((lats // 128,)),
            dma((chunks, 2)),
            dma((chunks, 2)),
            dma((chunks, 2, 2)),
            dma((chunks, 2, 2)),
            dma((NX - 1,)),
            dma((NX - 1,)),
            dma((chunks, NZ - 1)),
            dma((chunks, NZ - 1)),
            dma((NS - 1,)),
            dma((NS - 1,)),
            dma((NS - 1,)),
            dma((NS - 1,)),
        ],
        compiler_params=pltpu.CompilerParams(
            collective_id=0, has_side_effects=True, vmem_limit_bytes=61 * 2**20
        ),
    )(band_rows, wave_pairs, packer_order, field_bits, field_power, grid, jnp.transpose(legendre, (2, 0, 1)))


def solution(mesh):
    return jax.shard_map(
        shards,
        mesh=mesh,
        in_specs=(P(None, None, "ns", "ew"), P(), P(), P(), P(), P(), P("ns", None, None)),
        out_specs=P("ew", "ns", None, None),
        check_vma=False,
    )
```

```python
import functools

import jax
import jax.numpy as jnp
import numpy as np
from jax import lax
from jax.experimental import pallas as pl
from jax.experimental.pallas import tpu as pltpu
from jax.sharding import PartitionSpec as P

MESH = pl.DeviceIdType.MESH
NX = 4
NZ = 8
NS = 16
CH = 16
HALF = NZ * CH // 2
FAR_Z = (4, 3, 5, 2, 6, 1, 7)
FAR_NS = (8, 7, 9, 6, 10, 5, 11, 4, 12, 3, 13, 2, 14, 1, 15)
F32 = jnp.float32
BF16 = jnp.bfloat16


def _fit(function, terms):
    z = 0.125 + 0.125 * np.cos(np.pi * (np.arange(200) + 0.5) / 200)
    cheb = np.polynomial.chebyshev.Chebyshev.fit(z, function(np.sqrt(z)), terms - 1, domain=[0, 0.25])
    return [float(v) for v in cheb.convert(kind=np.polynomial.Polynomial).coef]


COS = _fit(lambda t: np.cos(2 * np.pi * t), 7)
SIN = _fit(lambda t: np.sin(2 * np.pi * t) / t, 7)


def _horner(coefs, z):
    total = jnp.full_like(z, coefs[-1])
    for c in coefs[-2::-1]:
        total = total * z + c
    return total


def _cos_sin(product, length, inverse):
    rest = product - jnp.round(product * inverse) * length
    t = rest * inverse
    z = t * t
    return _horner(COS, z), t * _horner(SIN, z)


def kernel(
    truncation, levels,
    band_hbm, waves_hbm, order_hbm, bits_hbm, power_hbm, grid_hbm, leg_hbm,
    out_ref,
    band_s, waves_s, order_s, bits_s, power_s,
    gridv0, gridv, legv, leghi, leglo, xf, w, cs, sbuf, rfar, rx, zbuf, rz, rz0, sum0, rx0, obuf, ybuf, ry, rmm,
    small_sem, grid_sem, leg_sem, fs_sem, fr_sem, xs_sem, xr_sem, x0s_sem, x0r_sem, zs_sem, zr_sem, ys_sem, yr_sem, ms_sem, mr_sem,
):
    ew, ns = lax.axis_index("ew"), lax.axis_index("ns")
    x, z = lax.rem(ew, NX), lax.div(ew, NX)
    rows, points = grid_hbm.shape[2:]
    chunks = rows // CH

    small_copies = [
        pltpu.make_async_copy(a, b, small_sem.at[i])
        for i, (a, b) in enumerate(
            ((waves_hbm, waves_s), (band_hbm, band_s), (order_hbm, order_s), (bits_hbm, bits_s), (power_hbm, power_s)))
    ]
    for copy in small_copies:
        copy.start()
    grid_copy0 = pltpu.make_async_copy(grid_hbm.at[:, :, 0:CH], gridv0, grid_sem.at[0])
    grid_copy0.start()
    grid_copy = pltpu.make_async_copy(grid_hbm.at[:, :, CH:rows], gridv, grid_sem.at[1])
    grid_copy.start()
    leg_copies = [
        pltpu.make_async_copy(leg_hbm.at[:, 0, k * 128 : (k + 1) * 128], legv.at[k], leg_sem.at[k])
        for k in range(legv.shape[0])
    ]
    for copy in leg_copies:
        copy.start()

    barrier = pltpu.get_barrier_semaphore()
    for d in FAR_NS:
        pl.semaphore_signal(barrier, inc=1, device_id={"ns": lax.rem(ns + d, NS)}, device_id_type=MESH)
    for d in FAR_Z:
        pl.semaphore_signal(barrier, inc=1, device_id={"ew": lax.rem(z + d, NZ) * NX + x}, device_id_type=MESH)
    for d in range(1, NX):
        pl.semaphore_signal(barrier, inc=1, device_id={"ew": z * NX + lax.rem(x + d, NX)}, device_id_type=MESH)

    w[...] = jnp.zeros_like(w)
    xf[1] = jnp.zeros_like(xf[1])

    for copy in small_copies:
        copy.wait()

    lane = lax.broadcasted_iota(jnp.int32, (16, 128), 1)
    sub16 = lax.broadcasted_iota(jnp.int32, (16, 128), 0)
    pair_of = (lane & 63) >> 2
    wave = jnp.zeros((16, 128), jnp.int32)
    for p in range(16):
        wave = jnp.where(pair_of == p, waves_s[p], wave)
    wave = jnp.where((lane & 2) == 0, wave, truncation - wave).astype(F32)
    imaginary = (lane & 1) == 1
    low_half = lane < 64
    first = ew * points
    product_a = wave * (first + 16 * sub16).astype(F32)
    product_b = wave * sub16.astype(F32)
    point0 = (first + sub16).astype(F32)
    point_end = (first + points).astype(F32)

    def neighbour(side):
        return lax.rem(x + (1 if side == 0 else NX - 1), NX)

    def far_copy(c, side):
        return pltpu.make_async_remote_copy(
            src_ref=sbuf.at[c, lax.rem(x + 2, NX), pl.ds(side * HALF, HALF)], dst_ref=rfar.at[c, side],
            send_sem=fs_sem.at[c, side], recv_sem=fr_sem.at[c, side],
            device_id={"ew": z * NX + neighbour(side)}, device_id_type=MESH)

    def near_copy(c, side, part):
        rows = pl.ds(part * HALF, HALF)
        return pltpu.make_async_remote_copy(
            src_ref=sbuf.at[c, neighbour(side), rows], dst_ref=rx.at[c, side, rows],
            send_sem=xs_sem.at[c, side, part], recv_sem=xr_sem.at[c, side, part],
            device_id={"ew": z * NX + neighbour(side)}, device_id_type=MESH)

    def z_copy(c, d):
        to = lax.rem(z + d, NZ)
        return pltpu.make_async_remote_copy(
            src_ref=zbuf.at[c, pl.ds(pl.multiple_of(to * CH, CH), CH)], dst_ref=rz.at[c, d - 1],
            send_sem=zs_sem.at[c, d - 1], recv_sem=zr_sem.at[c, d - 1],
            device_id={"ew": to * NX + x}, device_id_type=MESH)

    def y_copy(d):
        to = lax.rem(ns + d, NS)
        return pltpu.make_async_remote_copy(
            src_ref=ybuf.at[to], dst_ref=ry.at[ns],
            send_sem=ys_sem.at[d - 1], recv_sem=yr_sem.at[d - 1],
            device_id={"ns": to}, device_id_type=MESH)

    def m_copy(d):
        to = lax.rem(ns + d, NS)
        return pltpu.make_async_remote_copy(
            src_ref=rmm.at[0, 0:1], dst_ref=rmm.at[d, 0:1],
            send_sem=ms_sem.at[d - 1], recv_sem=mr_sem.at[d - 1],
            device_id={"ns": to}, device_id_type=MESH)

    def pass_on(c):
        for side in (0, 1):
            far_copy(c, side).wait_recv()
            rows = pl.ds(side * HALF, HALF)
            sbuf[c, neighbour(side), rows] = sbuf[c, neighbour(side), rows] + rfar[c, side]
            near_copy(c, side, side).start()

    def along_z(c):
        for side in (0, 1):
            for part in (0, 1):
                near_copy(c, side, part).wait_recv()
        zbuf[c] = sbuf[c, x] + rx[c, 0] + rx[c, 1]
        for d in FAR_Z:
            z_copy(c, d).start()

    def compute(c, grid_ref, grid_row):
        def convert(zz, _):
            for xx in range(NX):
                field = order_s[zz * NX + xx]
                for h in range(2):
                    at = pl.multiple_of((h * 32 + xx * NZ + zz) * CH, CH)
                    block = grid_ref[field, h, pl.ds(grid_row, CH), :].astype(F32)
                    xf[0, pl.ds(at, CH), :] = block[:, 0:128]
                    xf[1, pl.ds(at, CH), 0 : points - 128] = block[:, 128:points]
            return 0

        lax.fori_loop(0, NZ, convert, 0)

        def half(g, _):
            for j in range(4):
                row0 = g * 8 + j
                band0 = band_s[ns * rows + c * CH + row0]
                band1 = band_s[ns * rows + c * CH + row0 + 4]
                length = jnp.where(low_half, 20 + 4 * band0, 20 + 4 * band1).astype(F32)
                inverse = 1.0 / length
                cos_a, sin_a = _cos_sin(product_a, length, inverse)
                cos_b, sin_b = _cos_sin(product_b, length, inverse)
                cs[j, 0] = jnp.where(imaginary, -sin_a, cos_a) * inverse
                cs[j, 1] = jnp.where(imaginary, cos_a, sin_a) * inverse
                end = jnp.minimum(length, point_end) - point0
                for a in range(11):
                    value = cs[j, 0, a : a + 1, :] * cos_b - cs[j, 1, a : a + 1, :] * sin_b
                    value = jnp.where(end > 16.0 * a, value, 0.0)
                    high = value.astype(BF16)
                    low = (value - high.astype(F32)).astype(BF16)
                    w[j, 16 * a : 16 * a + 16, 0:128] = high
                    w[j, 16 * a : 16 * a + 16, 128:256] = low
                sides = []
                for side in range(2):
                    x0 = xf[side, pl.ds(row0, 64, stride=CH), :].astype(BF16)
                    x1 = xf[side, pl.ds(row0 + 4, 64, stride=CH), :].astype(BF16)
                    sides.append(jnp.concatenate([x0, x1], 0))
                both = jnp.dot(jnp.concatenate(sides, 1), w[j], preferred_element_type=F32)
                both = both[:, :128] + both[:, 128:]
                out = jnp.where(lax.broadcasted_iota(jnp.int32, (64, 128), 1) < 64, both[:64], both[64:])
                for h in range(2):
                    for xx in range(NX):
                        sbuf[c, xx, pl.ds(g * 8 + h * 4 + j, NZ, stride=CH), :] = out[h * 32 + xx * NZ : h * 32 + xx * NZ + NZ]
            return 0

        lax.fori_loop(0, CH // 8, half, 0)

    def first_z_copy(d):
        to = lax.rem(z + d, NZ)
        return pltpu.make_async_remote_copy(
            src_ref=sbuf.at[2, :, pl.ds(pl.multiple_of(to * CH, CH), CH)], dst_ref=rz0.at[d - 1],
            send_sem=zs_sem.at[2, d - 1], recv_sem=zr_sem.at[2, d - 1],
            device_id={"ew": to * NX + x}, device_id_type=MESH)

    def first_x_copy(d):
        to = lax.rem(x + d, NX)
        return pltpu.make_async_remote_copy(
            src_ref=sum0.at[to], dst_ref=rx0.at[d - 1],
            send_sem=x0s_sem.at[d - 1], recv_sem=x0r_sem.at[d - 1],
            device_id={"ew": z * NX + to}, device_id_type=MESH)

    grid_copy0.wait()
    compute(0, gridv0, 0)
    pl.semaphore_wait(barrier, NX - 1 + NZ - 1 + NS - 1)
    def send_x(c):
        for side in (0, 1):
            far_copy(c, side).start()
            near_copy(c, side, 1 - side).start()

    send_x(0)
    grid_copy.wait()
    compute(1, gridv, 0)
    send_x(1)
    compute(2, gridv, CH)
    for d in FAR_Z:
        first_z_copy(d).start()

    def chunk(c, _):
        compute(c, gridv, pl.multiple_of(c * CH - CH, CH))
        send_x(c)

        pass_on(c - 3)

        return 0

    lax.fori_loop(3, chunks, chunk, 0)

    pass_on(chunks - 2)
    along_z(0)
    pass_on(chunks - 1)
    along_z(1)
    for d in range(1, NZ):
        first_z_copy(d).wait_recv()
    total = sbuf[2, :, pl.ds(pl.multiple_of(z * CH, CH), CH), :]
    for d in range(NZ - 1):
        total = total + rz0[d]
    sum0[...] = total
    for d in range(1, NX):
        first_x_copy(d).start()

    def second(c, _):
        along_z(c)
        return 0

    lax.fori_loop(3, chunks, second, 0)

    for copy in leg_copies:
        copy.wait()

    def split(i, _):
        at = pl.ds(pl.multiple_of(i * 128, 128), 128)
        value = legv[i].T
        high = value.astype(BF16)
        leghi[at, :] = high
        leglo[at, :] = (value - high.astype(F32)).astype(BF16)
        return 0

    lax.fori_loop(0, legv.shape[0], split, 0)

    sub8 = lax.broadcasted_iota(jnp.int32, (8, 128), 0)
    lane8 = lax.broadcasted_iota(jnp.int32, (8, 128), 1)
    obuf[...] = jnp.zeros_like(obuf)

    def place(c, total):
        for g in range(CH // 8):
            o = total[g * 8 : g * 8 + 8]
            r = pltpu.roll(o, 4, 0)
            o = jnp.where(sub8 < 4, o + r, r - o)
            r = pltpu.roll(pltpu.roll(o, 4, 0), 64, 1)
            o = jnp.where((sub8 < 4) == (lane8 < 64), o, r)
            obuf[pl.ds(pl.multiple_of(c * CH + g * 8, 8), 8), :] = o

    for d in range(1, NX):
        first_x_copy(d).wait_recv()
    place(2, sum0[x] + rx0[0] + rx0[1] + rx0[2])

    def third(i, _):
        c = i + lax.div(i, 2)
        for d in range(1, NZ):
            z_copy(c, d).wait_recv()
        total = zbuf[c, pl.ds(pl.multiple_of(z * CH, CH), CH)]
        for d in range(NZ - 1):
            total = total + rz[c, d]
        place(c, total)
        return 0

    lax.fori_loop(0, chunks - 1, third, 0)

    turned = obuf[...].T
    for p in range(NS):
        ybuf[p] = jnp.concatenate([turned[4 * p : 4 * p + 4], turned[64 + 4 * p : 68 + 4 * p]], 0)
    for d in FAR_NS:
        y_copy(d).start()
    ry[ns] = ybuf[ns]

    columns = leghi.shape[1]
    column = lax.broadcasted_iota(jnp.int32, (2, columns), 1)
    wavenum = waves_s[ns]
    in_first = column <= truncation - wavenum
    shifted = jnp.where(in_first, column, column - (truncation - wavenum + 1))
    even = (shifted & 1) == 0
    degree = jnp.where(in_first, wavenum + column, column - 1).astype(F32)
    field_type = lax.div(order_s[ew], levels)
    power, bits = power_s[0], bits_s[0]
    for t in range(1, bits_s.shape[0]):
        power = jnp.where(field_type == t, power_s[t], power)
        bits = jnp.where(field_type == t, bits_s[t], bits)
    weight = jnp.exp(power * jnp.log(degree * (degree + 1.0) + 2.0))
    spread = (lax.shift_left(jnp.int32(1), bits) - 1).astype(F32) * (1.0 / 4096.0)

    def sent(i, _):
        c = i + lax.div(i, 2)
        for side in (0, 1):
            far_copy(c, side).wait_send()
            for part in (0, 1):
                near_copy(c, side, part).wait_send()
        for d in range(1, NZ):
            z_copy(c, d).wait_send()
        return 0

    lax.fori_loop(0, chunks - 1, sent, 0)
    for d in range(1, NZ):
        first_z_copy(d).wait_send()
    for d in range(1, NX):
        first_x_copy(d).wait_send()
    for d in range(1, NS):
        y_copy(d).wait_recv()
    pieces = [None] * (rows * NS // 128)
    for i in range(NS):
        at, off = divmod(i * rows, 128)
        value = ry[i] if off == 0 else pltpu.roll(ry[i], off, 1)
        if off + rows <= 128:
            parts = [(at, value)]
        else:
            parts = [(at, jnp.where(lane8 >= off, value, 0.0)), (at + 1, jnp.where(lane8 < off, value, 0.0))]
        for k, v in parts:
            pieces[k] = v if pieces[k] is None else pieces[k] + v
    stacked = jnp.concatenate(pieces, 1)
    high = stacked.astype(BF16).astype(F32)
    both = jnp.concatenate([high, stacked - high], 0).astype(BF16)
    by_high = jnp.dot(both, leghi[...], preferred_element_type=F32)
    by_low = jnp.dot(both, leglo[...], preferred_element_type=F32)
    result = by_high[:8] + by_high[8:] + by_low[:8]

    chosen = jnp.where(
        in_first,
        jnp.where(even, result[0:2], result[4:6]),
        jnp.where(even, result[2:4], result[6:8]),
    )
    scaled = chosen * weight
    most = jnp.max(jnp.max(scaled, axis=0, keepdims=True), axis=1, keepdims=True)
    least = jnp.min(jnp.min(scaled, axis=0, keepdims=True), axis=1, keepdims=True)
    rmm[0, 0:1] = jnp.where(lane8[0:1] < 64, most, -least)
    for d in FAR_NS:
        m_copy(d).start()
    for d in range(1, NS):
        y_copy(d).wait_send()
    for d in range(1, NS):
        m_copy(d).wait_recv()
    top = rmm[0, 0:1]
    for d in range(1, NS):
        top = jnp.maximum(top, rmm[d, 0:1])
    highest = top[:, 0:1]
    lowest = -top[:, 64:65]
    span = highest - lowest + 1e-6
    out_ref[0, 0] = (scaled - lowest) / span * spread

    for d in range(1, NS):
        m_copy(d).wait_send()


def shards(grid, band_rows, wave_pairs, packer_order, field_bits, field_power, legendre):
    fields, hemis, rows, points = grid.shape
    lats, columns = legendre.shape[1:]
    truncation = columns - 2
    levels = fields // field_bits.shape[0]
    chunks = rows // CH
    hbm = pl.BlockSpec(memory_space=pltpu.HBM)
    dma = pltpu.SemaphoreType.DMA
    return pl.pallas_call(
        functools.partial(kernel, truncation, levels),
        out_shape=jax.ShapeDtypeStruct((1, 1, 2, columns), F32),
        in_specs=[hbm] * 7,
        out_specs=pl.BlockSpec(memory_space=pltpu.VMEM),
        scratch_shapes=[
            pltpu.SMEM(band_rows.shape, jnp.int32),
            pltpu.SMEM(wave_pairs.shape, jnp.int32),
            pltpu.SMEM(packer_order.shape, jnp.int32),
            pltpu.SMEM(field_bits.shape, jnp.int32),
            pltpu.SMEM(field_power.shape, F32),
            pltpu.VMEM((fields, hemis, CH, points), BF16),
            pltpu.VMEM((fields, hemis, rows - CH, points), BF16),
            pltpu.VMEM((lats // 128, columns, 128), F32),
            pltpu.VMEM((lats, columns), BF16),
            pltpu.VMEM((lats, columns), BF16),
            pltpu.VMEM((2, fields * hemis * CH, 128), F32),
            pltpu.VMEM((4, 256, 256), BF16),
            pltpu.VMEM((4, 2, 16, 128), F32),
            pltpu.VMEM((chunks, NX, NZ * CH, 128), F32),
            pltpu.VMEM((chunks, 2, HALF, 128), F32),
            pltpu.VMEM((chunks, 2, NZ * CH, 128), F32),
            pltpu.VMEM((chunks, NZ * CH, 128), F32),
            pltpu.VMEM((chunks, NZ - 1, CH, 128), F32),
            pltpu.VMEM((NZ - 1, NX, CH, 128), F32),
            pltpu.VMEM((NX, CH, 128), F32),
            pltpu.VMEM((NX - 1, CH, 128), F32),
            pltpu.VMEM((128, 128), F32),
            pltpu.VMEM((NS, 8, 128), F32),
            pltpu.VMEM((NS, 8, 128), F32),
            pltpu.VMEM((NS, 8, 128), F32),
            dma((5,)),
            dma((2,)),
            dma((lats // 128,)),
            dma((chunks, 2)),
            dma((chunks, 2)),
            dma((chunks, 2, 2)),
            dma((chunks, 2, 2)),
            dma((NX - 1,)),
            dma((NX - 1,)),
            dma((chunks, NZ - 1)),
            dma((chunks, NZ - 1)),
            dma((NS - 1,)),
            dma((NS - 1,)),
            dma((NS - 1,)),
            dma((NS - 1,)),
        ],
        compiler_params=pltpu.CompilerParams(
            collective_id=0, has_side_effects=True, vmem_limit_bytes=61 * 2**20
        ),
    )(band_rows, wave_pairs, packer_order, field_bits, field_power, grid, jnp.transpose(legendre, (2, 0, 1)))


def solution(mesh):
    return jax.shard_map(
        shards,
        mesh=mesh,
        in_specs=(P(None, None, "ns", "ew"), P(), P(), P(), P(), P(), P("ns", None, None)),
        out_specs=P("ew", "ns", None, None),
        check_vma=False,
    )
```

```python
import functools

import jax
import jax.numpy as jnp
import numpy as np
from jax import lax
from jax.experimental import pallas as pl
from jax.experimental.pallas import tpu as pltpu
from jax.sharding import PartitionSpec as P

MESH = pl.DeviceIdType.MESH
NX = 4
NZ = 8
NS = 16
CH = 16
HALF = NZ * CH // 2
FAR_Z = (4, 3, 5, 2, 6, 1, 7)
FAR_NS = (8, 7, 9, 6, 10, 5, 11, 4, 12, 3, 13, 2, 14, 1, 15)
F32 = jnp.float32
BF16 = jnp.bfloat16


def _fit(function, terms):
    z = 0.125 + 0.125 * np.cos(np.pi * (np.arange(200) + 0.5) / 200)
    cheb = np.polynomial.chebyshev.Chebyshev.fit(z, function(np.sqrt(z)), terms - 1, domain=[0, 0.25])
    return [float(v) for v in cheb.convert(kind=np.polynomial.Polynomial).coef]


COS = _fit(lambda t: np.cos(2 * np.pi * t), 7)
SIN = _fit(lambda t: np.sin(2 * np.pi * t) / t, 7)


def _horner(coefs, z):
    total = jnp.full_like(z, coefs[-1])
    for c in coefs[-2::-1]:
        total = total * z + c
    return total


def _cos_sin(product, length, inverse):
    rest = product - jnp.round(product * inverse) * length
    t = rest * inverse
    z = t * t
    return _horner(COS, z), t * _horner(SIN, z)


def kernel(
    truncation, levels,
    band_hbm, waves_hbm, order_hbm, bits_hbm, power_hbm, grid_hbm, leg_hbm,
    out_ref,
    band_s, waves_s, order_s, bits_s, power_s,
    gridv0, gridv, legv, leghi, leglo, xf, w, cs, sbuf, rfar, rx, zbuf, rz, rz0, sum0, rx0, obuf, ybuf, ry, rmm,
    small_sem, grid_sem, leg_sem, fs_sem, fr_sem, xs_sem, xr_sem, x0s_sem, x0r_sem, zs_sem, zr_sem, ys_sem, yr_sem, ms_sem, mr_sem,
):
    ew, ns = lax.axis_index("ew"), lax.axis_index("ns")
    x, z = lax.rem(ew, NX), lax.div(ew, NX)
    rows, points = grid_hbm.shape[2:]
    chunks = rows // CH

    small_copies = [
        pltpu.make_async_copy(a, b, small_sem.at[i])
        for i, (a, b) in enumerate(
            ((waves_hbm, waves_s), (band_hbm, band_s), (order_hbm, order_s), (bits_hbm, bits_s), (power_hbm, power_s)))
    ]
    for copy in small_copies:
        copy.start()
    grid_copy0 = pltpu.make_async_copy(grid_hbm.at[:, :, 0:CH], gridv0, grid_sem.at[0])
    grid_copy0.start()
    grid_copy = pltpu.make_async_copy(grid_hbm.at[:, :, CH:rows], gridv, grid_sem.at[1])
    grid_copy.start()
    leg_copies = [
        pltpu.make_async_copy(leg_hbm.at[:, 0, k * 128 : (k + 1) * 128], legv.at[k], leg_sem.at[k])
        for k in range(legv.shape[0])
    ]
    for copy in leg_copies:
        copy.start()

    barrier = pltpu.get_barrier_semaphore()
    for d in FAR_NS:
        pl.semaphore_signal(barrier, inc=1, device_id={"ns": lax.rem(ns + d, NS)}, device_id_type=MESH)
    for d in FAR_Z:
        pl.semaphore_signal(barrier, inc=1, device_id={"ew": lax.rem(z + d, NZ) * NX + x}, device_id_type=MESH)
    for d in range(1, NX):
        pl.semaphore_signal(barrier, inc=1, device_id={"ew": z * NX + lax.rem(x + d, NX)}, device_id_type=MESH)

    w[...] = jnp.zeros_like(w)
    xf[1] = jnp.zeros_like(xf[1])

    for copy in small_copies:
        copy.wait()

    lane = lax.broadcasted_iota(jnp.int32, (16, 128), 1)
    sub16 = lax.broadcasted_iota(jnp.int32, (16, 128), 0)
    pair_of = (lane & 63) >> 2
    wave = jnp.zeros((16, 128), jnp.int32)
    for p in range(16):
        wave = jnp.where(pair_of == p, waves_s[p], wave)
    wave = jnp.where((lane & 2) == 0, wave, truncation - wave).astype(F32)
    imaginary = (lane & 1) == 1
    low_half = lane < 64
    first = ew * points
    product_a = wave * (first + 16 * sub16).astype(F32)
    product_b = wave * sub16.astype(F32)
    point0 = (first + sub16).astype(F32)
    point_end = (first + points).astype(F32)

    def neighbour(side):
        return lax.rem(x + (1 if side == 0 else NX - 1), NX)

    def far_copy(c, side):
        return pltpu.make_async_remote_copy(
            src_ref=sbuf.at[c, lax.rem(x + 2, NX), pl.ds(side * HALF, HALF)], dst_ref=rfar.at[c, side],
            send_sem=fs_sem.at[c, side], recv_sem=fr_sem.at[c, side],
            device_id={"ew": z * NX + neighbour(side)}, device_id_type=MESH)

    def near_copy(c, side, part):
        rows = pl.ds(part * HALF, HALF)
        return pltpu.make_async_remote_copy(
            src_ref=sbuf.at[c, neighbour(side), rows], dst_ref=rx.at[c, side, rows],
            send_sem=xs_sem.at[c, side, part], recv_sem=xr_sem.at[c, side, part],
            device_id={"ew": z * NX + neighbour(side)}, device_id_type=MESH)

    def z_copy(c, d):
        to = lax.rem(z + d, NZ)
        return pltpu.make_async_remote_copy(
            src_ref=zbuf.at[c, pl.ds(pl.multiple_of(to * CH, CH), CH)], dst_ref=rz.at[c, d - 1],
            send_sem=zs_sem.at[c, d - 1], recv_sem=zr_sem.at[c, d - 1],
            device_id={"ew": to * NX + x}, device_id_type=MESH)

    def y_copy(d):
        to = lax.rem(ns + d, NS)
        return pltpu.make_async_remote_copy(
            src_ref=ybuf.at[to], dst_ref=ry.at[ns],
            send_sem=ys_sem.at[d - 1], recv_sem=yr_sem.at[d - 1],
            device_id={"ns": to}, device_id_type=MESH)

    def m_copy(d):
        to = lax.rem(ns + d, NS)
        return pltpu.make_async_remote_copy(
            src_ref=rmm.at[0, 0:1], dst_ref=rmm.at[d, 0:1],
            send_sem=ms_sem.at[d - 1], recv_sem=mr_sem.at[d - 1],
            device_id={"ns": to}, device_id_type=MESH)

    def pass_on(c):
        for side in (0, 1):
            far_copy(c, side).wait_recv()
            rows = pl.ds(side * HALF, HALF)
            sbuf[c, neighbour(side), rows] = sbuf[c, neighbour(side), rows] + rfar[c, side]
            near_copy(c, side, side).start()

    def along_z(c):
        for side in (0, 1):
            for part in (0, 1):
                near_copy(c, side, part).wait_recv()
        zbuf[c] = sbuf[c, x] + rx[c, 0] + rx[c, 1]
        for d in FAR_Z:
            z_copy(c, d).start()

    def compute(c, grid_ref, grid_row):
        def convert(zz, _):
            for xx in range(NX):
                field = order_s[zz * NX + xx]
                for h in range(2):
                    at = pl.multiple_of((h * 32 + xx * NZ + zz) * CH, CH)
                    block = grid_ref[field, h, pl.ds(grid_row, CH), :].astype(F32)
                    xf[0, pl.ds(at, CH), :] = block[:, 0:128]
                    xf[1, pl.ds(at, CH), 0 : points - 128] = block[:, 128:points]
            return 0

        lax.fori_loop(0, NZ, convert, 0)

        def half(g, _):
            for j in range(4):
                row0 = g * 8 + j
                band0 = band_s[ns * rows + c * CH + row0]
                band1 = band_s[ns * rows + c * CH + row0 + 4]
                length = jnp.where(low_half, 20 + 4 * band0, 20 + 4 * band1).astype(F32)
                inverse = 1.0 / length
                cos_a, sin_a = _cos_sin(product_a, length, inverse)
                cos_b, sin_b = _cos_sin(product_b, length, inverse)
                cs[j, 0] = jnp.where(imaginary, -sin_a, cos_a) * inverse
                cs[j, 1] = jnp.where(imaginary, cos_a, sin_a) * inverse
                end = jnp.minimum(length, point_end) - point0
                for a in range(11):
                    value = cs[j, 0, a : a + 1, :] * cos_b - cs[j, 1, a : a + 1, :] * sin_b
                    value = jnp.where(end > 16.0 * a, value, 0.0)
                    high = value.astype(BF16)
                    low = (value - high.astype(F32)).astype(BF16)
                    w[j, 16 * a : 16 * a + 16, 0:128] = high
                    w[j, 16 * a : 16 * a + 16, 128:256] = low
                sides = []
                for side in range(2):
                    x0 = xf[side, pl.ds(row0, 64, stride=CH), :].astype(BF16)
                    x1 = xf[side, pl.ds(row0 + 4, 64, stride=CH), :].astype(BF16)
                    sides.append(jnp.concatenate([x0, x1], 0))
                both = jnp.dot(jnp.concatenate(sides, 1), w[j], preferred_element_type=F32)
                both = both[:, :128] + both[:, 128:]
                out = jnp.where(lax.broadcasted_iota(jnp.int32, (64, 128), 1) < 64, both[:64], both[64:])
                for h in range(2):
                    for xx in range(NX):
                        sbuf[c, xx, pl.ds(g * 8 + h * 4 + j, NZ, stride=CH), :] = out[h * 32 + xx * NZ : h * 32 + xx * NZ + NZ]
            return 0

        lax.fori_loop(0, CH // 8, half, 0)

    def first_z_copy(d):
        to = lax.rem(z + d, NZ)
        return pltpu.make_async_remote_copy(
            src_ref=sbuf.at[2, :, pl.ds(pl.multiple_of(to * CH, CH), CH)], dst_ref=rz0.at[d - 1],
            send_sem=zs_sem.at[2, d - 1], recv_sem=zr_sem.at[2, d - 1],
            device_id={"ew": to * NX + x}, device_id_type=MESH)

    def first_x_copy(d):
        to = lax.rem(x + d, NX)
        return pltpu.make_async_remote_copy(
            src_ref=sum0.at[to], dst_ref=rx0.at[d - 1],
            send_sem=x0s_sem.at[d - 1], recv_sem=x0r_sem.at[d - 1],
            device_id={"ew": z * NX + to}, device_id_type=MESH)

    grid_copy0.wait()
    compute(0, gridv0, 0)
    pl.semaphore_wait(barrier, NX - 1 + NZ - 1 + NS - 1)
    def send_x(c):
        for side in (0, 1):
            far_copy(c, side).start()
            near_copy(c, side, 1 - side).start()

    send_x(0)
    grid_copy.wait()
    compute(1, gridv, 0)
    send_x(1)
    compute(2, gridv, CH)
    for d in FAR_Z:
        first_z_copy(d).start()

    def chunk(c, _):
        compute(c, gridv, pl.multiple_of(c * CH - CH, CH))
        send_x(c)

        pass_on(c - 3)

        return 0

    lax.fori_loop(3, chunks, chunk, 0)

    pass_on(chunks - 2)
    along_z(0)
    pass_on(chunks - 1)
    along_z(1)
    along_z(3)
    for d in range(1, NZ):
        first_z_copy(d).wait_recv()
    total = sbuf[2, :, pl.ds(pl.multiple_of(z * CH, CH), CH), :]
    for d in range(NZ - 1):
        total = total + rz0[d]
    sum0[...] = total
    for d in range(1, NX):
        first_x_copy(d).start()

    def second(c, _):
        along_z(c)
        return 0

    lax.fori_loop(4, chunks, second, 0)

    for copy in leg_copies:
        copy.wait()

    def split(i, _):
        at = pl.ds(pl.multiple_of(i * 128, 128), 128)
        value = legv[i].T
        high = value.astype(BF16)
        leghi[at, :] = high
        leglo[at, :] = (value - high.astype(F32)).astype(BF16)
        return 0

    lax.fori_loop(0, legv.shape[0], split, 0)

    sub8 = lax.broadcasted_iota(jnp.int32, (8, 128), 0)
    lane8 = lax.broadcasted_iota(jnp.int32, (8, 128), 1)
    obuf[...] = jnp.zeros_like(obuf)

    def place(c, total):
        for g in range(CH // 8):
            o = total[g * 8 : g * 8 + 8]
            r = pltpu.roll(o, 4, 0)
            o = jnp.where(sub8 < 4, o + r, r - o)
            r = pltpu.roll(pltpu.roll(o, 4, 0), 64, 1)
            o = jnp.where((sub8 < 4) == (lane8 < 64), o, r)
            obuf[pl.ds(pl.multiple_of(c * CH + g * 8, 8), 8), :] = o

    for d in range(1, NX):
        first_x_copy(d).wait_recv()
    place(2, sum0[x] + rx0[0] + rx0[1] + rx0[2])

    def third(i, _):
        c = i + lax.div(i, 2)
        for d in range(1, NZ):
            z_copy(c, d).wait_recv()
        total = zbuf[c, pl.ds(pl.multiple_of(z * CH, CH), CH)]
        for d in range(NZ - 1):
            total = total + rz[c, d]
        place(c, total)
        return 0

    lax.fori_loop(0, chunks - 1, third, 0)

    turned = obuf[...].T
    for p in range(NS):
        ybuf[p] = jnp.concatenate([turned[4 * p : 4 * p + 4], turned[64 + 4 * p : 68 + 4 * p]], 0)
    for d in FAR_NS:
        y_copy(d).start()
    ry[ns] = ybuf[ns]

    columns = leghi.shape[1]
    column = lax.broadcasted_iota(jnp.int32, (2, columns), 1)
    wavenum = waves_s[ns]
    in_first = column <= truncation - wavenum
    shifted = jnp.where(in_first, column, column - (truncation - wavenum + 1))
    even = (shifted & 1) == 0
    degree = jnp.where(in_first, wavenum + column, column - 1).astype(F32)
    field_type = lax.div(order_s[ew], levels)
    power, bits = power_s[0], bits_s[0]
    for t in range(1, bits_s.shape[0]):
        power = jnp.where(field_type == t, power_s[t], power)
        bits = jnp.where(field_type == t, bits_s[t], bits)
    weight = jnp.exp(power * jnp.log(degree * (degree + 1.0) + 2.0))
    spread = (lax.shift_left(jnp.int32(1), bits) - 1).astype(F32) * (1.0 / 4096.0)

    def sent(i, _):
        c = i + lax.div(i, 2)
        for side in (0, 1):
            far_copy(c, side).wait_send()
            for part in (0, 1):
                near_copy(c, side, part).wait_send()
        for d in range(1, NZ):
            z_copy(c, d).wait_send()
        return 0

    lax.fori_loop(0, chunks - 1, sent, 0)
    for d in range(1, NZ):
        first_z_copy(d).wait_send()
    for d in range(1, NX):
        first_x_copy(d).wait_send()
    for d in range(1, NS):
        y_copy(d).wait_recv()
    pieces = [None] * (rows * NS // 128)
    for i in range(NS):
        at, off = divmod(i * rows, 128)
        value = ry[i] if off == 0 else pltpu.roll(ry[i], off, 1)
        if off + rows <= 128:
            parts = [(at, value)]
        else:
            parts = [(at, jnp.where(lane8 >= off, value, 0.0)), (at + 1, jnp.where(lane8 < off, value, 0.0))]
        for k, v in parts:
            pieces[k] = v if pieces[k] is None else pieces[k] + v
    stacked = jnp.concatenate(pieces, 1)
    high = stacked.astype(BF16).astype(F32)
    both = jnp.concatenate([high, stacked - high], 0).astype(BF16)
    by_high = jnp.dot(both, leghi[...], preferred_element_type=F32)
    by_low = jnp.dot(both, leglo[...], preferred_element_type=F32)
    result = by_high[:8] + by_high[8:] + by_low[:8]

    chosen = jnp.where(
        in_first,
        jnp.where(even, result[0:2], result[4:6]),
        jnp.where(even, result[2:4], result[6:8]),
    )
    scaled = chosen * weight
    most = jnp.max(jnp.max(scaled, axis=0, keepdims=True), axis=1, keepdims=True)
    least = jnp.min(jnp.min(scaled, axis=0, keepdims=True), axis=1, keepdims=True)
    rmm[0, 0:1] = jnp.where(lane8[0:1] < 64, most, -least)
    for d in FAR_NS:
        m_copy(d).start()
    for d in range(1, NS):
        y_copy(d).wait_send()
    for d in range(1, NS):
        m_copy(d).wait_recv()
    top = rmm[0, 0:1]
    for d in range(1, NS):
        top = jnp.maximum(top, rmm[d, 0:1])
    highest = top[:, 0:1]
    lowest = -top[:, 64:65]
    span = highest - lowest + 1e-6
    out_ref[0, 0] = (scaled - lowest) / span * spread

    for d in range(1, NS):
        m_copy(d).wait_send()


def shards(grid, band_rows, wave_pairs, packer_order, field_bits, field_power, legendre):
    fields, hemis, rows, points = grid.shape
    lats, columns = legendre.shape[1:]
    truncation = columns - 2
    levels = fields // field_bits.shape[0]
    chunks = rows // CH
    hbm = pl.BlockSpec(memory_space=pltpu.HBM)
    dma = pltpu.SemaphoreType.DMA
    return pl.pallas_call(
        functools.partial(kernel, truncation, levels),
        out_shape=jax.ShapeDtypeStruct((1, 1, 2, columns), F32),
        in_specs=[hbm] * 7,
        out_specs=pl.BlockSpec(memory_space=pltpu.VMEM),
        scratch_shapes=[
            pltpu.SMEM(band_rows.shape, jnp.int32),
            pltpu.SMEM(wave_pairs.shape, jnp.int32),
            pltpu.SMEM(packer_order.shape, jnp.int32),
            pltpu.SMEM(field_bits.shape, jnp.int32),
            pltpu.SMEM(field_power.shape, F32),
            pltpu.VMEM((fields, hemis, CH, points), BF16),
            pltpu.VMEM((fields, hemis, rows - CH, points), BF16),
            pltpu.VMEM((lats // 128, columns, 128), F32),
            pltpu.VMEM((lats, columns), BF16),
            pltpu.VMEM((lats, columns), BF16),
            pltpu.VMEM((2, fields * hemis * CH, 128), F32),
            pltpu.VMEM((4, 256, 256), BF16),
            pltpu.VMEM((4, 2, 16, 128), F32),
            pltpu.VMEM((chunks, NX, NZ * CH, 128), F32),
            pltpu.VMEM((chunks, 2, HALF, 128), F32),
            pltpu.VMEM((chunks, 2, NZ * CH, 128), F32),
            pltpu.VMEM((chunks, NZ * CH, 128), F32),
            pltpu.VMEM((chunks, NZ - 1, CH, 128), F32),
            pltpu.VMEM((NZ - 1, NX, CH, 128), F32),
            pltpu.VMEM((NX, CH, 128), F32),
            pltpu.VMEM((NX - 1, CH, 128), F32),
            pltpu.VMEM((128, 128), F32),
            pltpu.VMEM((NS, 8, 128), F32),
            pltpu.VMEM((NS, 8, 128), F32),
            pltpu.VMEM((NS, 8, 128), F32),
            dma((5,)),
            dma((2,)),
            dma((lats // 128,)),
            dma((chunks, 2)),
            dma((chunks, 2)),
            dma((chunks, 2, 2)),
            dma((chunks, 2, 2)),
            dma((NX - 1,)),
            dma((NX - 1,)),
            dma((chunks, NZ - 1)),
            dma((chunks, NZ - 1)),
            dma((NS - 1,)),
            dma((NS - 1,)),
            dma((NS - 1,)),
            dma((NS - 1,)),
        ],
        compiler_params=pltpu.CompilerParams(
            collective_id=0, has_side_effects=True, vmem_limit_bytes=61 * 2**20
        ),
    )(band_rows, wave_pairs, packer_order, field_bits, field_power, grid, jnp.transpose(legendre, (2, 0, 1)))


def solution(mesh):
    return jax.shard_map(
        shards,
        mesh=mesh,
        in_specs=(P(None, None, "ns", "ew"), P(), P(), P(), P(), P(), P("ns", None, None)),
        out_specs=P("ew", "ns", None, None),
        check_vma=False,
    )
```
